768 devices in a mesh: lon: 96 (over z, y_hi, x), lat: 8 (over y_lo, core).
Axes of the slice: x: 4, y: 8 (y_hi: 2, y_lo: 4; y = y_hi * 4 + y_lo), z: 12, core: 2. Of those that a mesh axis runs over, the one named last changes fastest.
Arguments:
- right_side: float32 [70, 384, 1024], P(None, 'lon', 'lat'), may hold values from -12 to 12
- first_guess: float32 [70, 384, 1024], P(None, 'lon', 'lat'), may hold values from -1.8 to 1.8
- cell_scale: float32 [70, 384, 1024], P(None, 'lon', 'lat'), may hold values from 0.6 to 1.6
- helmholtz_term: float32 [70, 384, 1024], P(None, 'lon', 'lat'), may hold values from 0.05 to 0.5
- vertical_coupling: float32 [69], replicated, may hold values from 0.5 to 4
Outputs:
- solution: float32 [70, 384, 1024], P(None, 'lon', 'lat')
- residual: float32 [70, 384, 1024], P(None, 'lon', 'lat')
The draws below stay inside these ranges and needn't reach their ends.
All inputs are finite; a program needn't handle non-finite values.
Results may differ from the reference program's by a relative error of at most 0.00026.
Values sent between devices are 32-bit elements; how exact they have to be, the bound alone decides.
A program may use at most 32 MiB of HBM per device.

```python
import math
import jax
import jax.numpy as jnp

LEV = 70
ITERS = 2
NLON = 384
NLAT = 1024


def draw_right_side(key, part):
    lon_pos = jnp.arange(NLON, dtype=jnp.float32)
    ramp_factor = 1.0 + 2.0 * lon_pos / (NLON - 1)
    rough_part = jax.random.truncated_normal(key, -4.0, 4.0, (LEV, NLON, NLAT), jnp.float32)
    return rough_part * ramp_factor[None, :, None]


def shard_levels(key, shape, split, low, top_value):
    factor_of = 1.0
    for dim, blocks in split:
        draws = jax.random.uniform(jax.random.fold_in(jax.random.fold_in(key, 6), dim), (blocks,), jnp.float32, low / len(split), top_value / len(split))
        factor_of = factor_of * jnp.repeat(jnp.exp(draws), shape[dim] // blocks).reshape((-1,) + (1,) * (len(shape) - 1 - dim))
    return factor_of


def noise(rng, dims, deviation, reach, pieces=(), kind=jnp.bfloat16):
    factor_of = shard_levels(rng, dims, pieces, -0.22, 0.18) if pieces else 1.0
    values = jax.random.normal(rng, dims, jnp.float32) * deviation * factor_of
    return jnp.minimum(jnp.maximum(values, -reach), reach).astype(kind)


def setup_inputs(seed: int = 0) -> dict:
    streams_of = jax.random.split(jax.random.key(seed), 6)
    return {
        "right_side": draw_right_side(jax.random.fold_in(streams_of[5], 71), 0),
        "first_guess": noise(streams_of[1], (LEV, NLON, NLAT), 0.3, 1.8, ((1, 96), (2, 8)), jnp.float32),
        "cell_scale": jnp.clip(jnp.exp(math.log(1.6) - 0.98082923 * jax.random.uniform(streams_of[2], (LEV, NLON, NLAT), jnp.float32) ** shard_levels(streams_of[2], (LEV, NLON, NLAT), ((1, 96), (2, 8)), -0.2, 0.2)), 0.6, 1.6),
        "helmholtz_term": jnp.clip(jnp.exp(math.log(0.5) - 2.3025851 * jax.random.uniform(streams_of[3], (LEV, NLON, NLAT), jnp.float32) ** shard_levels(streams_of[3], (LEV, NLON, NLAT), ((1, 96), (2, 8)), -0.2, 0.2)), 0.05, 0.5),
        "vertical_coupling": jnp.clip(jnp.exp(jax.random.uniform(streams_of[4], (LEV - 1,), jnp.float32, math.log(0.5), math.log(4.0))), 0.5, 4.0),
    }


def operator_apply(field, cell_scale, helmholtz_term, vertical_coupling):
    half_cycle = field.shape[1] // 2
    scaled = cell_scale * field
    east_side = jnp.roll(scaled, -1, axis=1)
    west_side = jnp.roll(scaled, 1, axis=1)
    north_edge = jnp.roll(scaled[:, :, :1], half_cycle, axis=1)
    south_edge = jnp.roll(scaled[:, :, -1:], half_cycle, axis=1)
    north_side = jnp.concatenate([north_edge, scaled[:, :, :-1]], axis=2)
    south_side = jnp.concatenate([scaled[:, :, 1:], south_edge], axis=2)
    horizontal = (4.0 + helmholtz_term) * scaled - east_side - west_side - north_side - south_side
    vert_flux = vertical_coupling[:, None, None] * (scaled[:-1] - scaled[1:])
    zero_layer = jnp.zeros_like(scaled[:1])
    vertical = jnp.concatenate([vert_flux, zero_layer], axis=0) - jnp.concatenate([zero_layer, vert_flux], axis=0)
    return cell_scale * (horizontal + vertical)


def reference(right_side, first_guess, cell_scale, helmholtz_term, vertical_coupling):
    def apply_operator(field):
        return operator_apply(field, cell_scale, helmholtz_term, vertical_coupling)

    solution = first_guess
    residual = right_side - apply_operator(first_guess)
    shadow = residual
    direction = residual
    rho_now = jnp.sum(residual * residual)
    for iteration in range(ITERS):
        image_vec = apply_operator(direction)
        alpha_step = rho_now / jnp.sum(shadow * image_vec)
        half_step = residual - alpha_step * image_vec
        second_image = apply_operator(half_step)
        omega_step = jnp.sum(second_image * half_step) / jnp.sum(second_image * second_image)
        solution = solution + alpha_step * direction + omega_step * half_step
        residual = half_step - omega_step * second_image
        if iteration + 1 < ITERS:
            rho_next = jnp.sum(shadow * half_step) - omega_step * jnp.sum(shadow * second_image)
            beta_step = (rho_next / rho_now) * (alpha_step / omega_step)
            direction = residual + beta_step * (direction - omega_step * image_vec)
            rho_now = rho_next
    return solution, residual
```

```python
import jax
import jax.numpy as jnp
from jax import lax
from jax.experimental import pallas as pl
from jax.experimental.pallas import tpu as pltpu
from jax.sharding import PartitionSpec as P

MESH = pl.DeviceIdType.MESH
F32 = jnp.float32

LEV = 70
GROUP = 16
GROUPS = 5
PAD = GROUP * GROUPS
ROWS = 4
NX, NYH, NZ, NYL, NC = 4, 2, 12, 4, 2
NLONB, NBAND = NX * NYH * NZ, NYL * NC
SIZE_A, SIZE_B = NX * NYH * NYL, NZ * NC


def two_sum(a, b):
    s = a + b
    t = s - a
    return s, (a - (s - t)) + (b - t)


def quick_two_sum(a, b):
    s = a + b
    return s, b - (s - a)


def split(a):
    c = 4097.0 * a
    high = c - (c - a)
    return high, a - high


def two_prod(a, b):
    p = a * b
    ah, al = split(a)
    bh, bl = split(b)
    return p, ((ah * bh - p) + ah * bl + al * bh) + al * bl


def dd_add(a, b):
    s, e = two_sum(a[0], b[0])
    return quick_two_sum(s, e + (a[1] + b[1]))


def dd_neg(a):
    return -a[0], -a[1]


def dd_sub(a, b):
    return dd_add(a, dd_neg(b))


def dd_mul(a, b):
    p, e = two_prod(a[0], b[0])
    return quick_two_sum(p, e + (a[0] * b[1] + a[1] * b[0]))


def dd_div(a, b):
    q = a[0] / b[0]
    zero = jnp.zeros_like(q)
    r = dd_sub(a, dd_mul((q, zero), b))
    return quick_two_sum(q, r[0] / b[0])


def roll(x, shift, axis):
    return pltpu.roll(x, shift % x.shape[axis], axis)


def halo_peers():
    lon, band = lax.axis_index("lon"), lax.axis_index("lat")
    west, east = lax.rem(lon + NLONB - 1, NLONB), lax.rem(lon + 1, NLONB)
    first = 1 - jnp.minimum(band, 1)
    last = jnp.maximum(band, NBAND - 2) - (NBAND - 2)

    def across(index, pole):
        return lax.rem(index + pole * (NLONB // 2), NLONB)

    left_band, right_band = band - 1 + first, band + 1 - last
    beside = ((west, band), (east, band))
    left = tuple((across(i, first), left_band) for i in (lon, west, east))
    right = tuple((across(i, last), right_band) for i in (lon, west, east))
    return beside, left, right, first, last


def sum_peers():
    lon, band = lax.axis_index("lon"), lax.axis_index("lat")
    x, y_hi, z = lax.rem(lon, NX), lax.rem(lon // NX, NYH), lon // (NX * NYH)
    core, y_lo = lax.rem(band, NC), band // NC
    me_a = (y_hi * NYL + y_lo) * NX + x
    me_b = z * NC + core
    group_a, group_b = [], []
    for j in range(1, SIZE_A):
        t = lax.rem(me_a + j, SIZE_A)
        px, py = lax.rem(t, NX), t // NX
        group_a.append(((z * NYH + py // NYL) * NX + px, lax.rem(py, NYL) * NC + core))
    for j in range(1, SIZE_B):
        t = lax.rem(me_b + j, SIZE_B)
        pc, pz = lax.rem(t, NC), t // NC
        group_b.append(((pz * NYH + y_hi) * NX + x, y_lo * NC + pc))
    return (me_a, group_a), (me_b, group_b)


def kernel(
    b_hbm, x_hbm, d_hbm, h_hbm, vc, sol_hbm, res_hbm,
    b_in, x_in, d_in, h_in, d_c, h_c, d_o, h_o,
    q_a, q_b, q_c, q_d, o_a, o_b,
    near, wide, vs, packed, ext1, ext2, ex, ey, sums_a, sums_b, row_a, row_b, couple, sol, res,
    load_sem, send1, recv1, send1x, recv1x, send2, recv2, send2x, recv2x, send_a, recv_a, send_b, recv_b,
):
    beside, left, right, first, last = halo_peers()
    (me_a, group_a), (me_b, group_b) = sum_peers()

    loads = [
        pltpu.make_async_copy(src, dst.at[pl.ds(0, LEV), pl.ds(2, ROWS)], load_sem.at[i])
        for i, (src, dst) in enumerate(((d_hbm, d_in), (x_hbm, x_in), (h_hbm, h_in), (b_hbm, b_in)))
    ]
    for copy in loads:
        copy.start()

    barrier = pltpu.get_barrier_semaphore()
    peers = [*beside, *left, *right, *group_a, *group_b]
    for peer in peers:
        pl.semaphore_signal(barrier, inc=1, device_id=peer, device_id_type=MESH)

    lane = lax.broadcasted_iota(jnp.int32, (8, 128), 1)
    sub = lax.broadcasted_iota(jnp.int32, (8, 128), 0)
    lane5 = lax.broadcasted_iota(jnp.int32, (GROUPS, 8, 128), 2)
    sub5 = lax.broadcasted_iota(jnp.int32, (GROUPS, 8, 128), 1)
    col5 = lax.rem(lane5, 8)
    is_own = (sub >= 2) & (sub < 6)

    tail = jnp.zeros((PAD - LEV, 8, 128), F32)
    for ref in (b_in, x_in, d_in, h_in, near):
        ref[LEV:PAD] = tail
    for i in range(3):
        for j in range(2):
            wide[i, j, LEV:PAD] = tail
    for ref in (q_a, q_b, q_c, q_d, o_a, o_b):
        ref[0] = jnp.zeros((8, 128), F32)
        ref[PAD + 1] = jnp.zeros((8, 128), F32)

    for k in range(PAD + 2):
        couple[k] = vc[k - 1] if 1 <= k < LEV else jnp.float32(0.0)

    def levels(step, init):
        def group(p, carry):
            return step(p, carry)

        return lax.fori_loop(0, GROUPS, group, init)

    def pack_in(tile, value, i):
        return jnp.where((lane >= 8 * i) & (lane < 8 * i + 8), roll(value, 8 * i + 4, 1), tile)

    def pack_field(ref, slot, at):
        def step(p, _):
            tile = jnp.zeros((8, 128), F32)
            for i in range(GROUP):
                tile = pack_in(tile, ref[p * GROUP + i + at], i)
            packed[slot, p] = tile
            return 0

        levels(step, 0)

    loads[0].wait()
    loads[1].wait()

    def scaled_guess(p, _):
        tile = jnp.zeros((8, 128), F32)
        for i in range(GROUP):
            k = p * GROUP + i
            value = d_in[k] * x_in[k]
            q_a[k + 1] = value
            tile = pack_in(tile, value, i)
        packed[0, p] = tile
        return 0

    levels(scaled_guess, 0)

    def remote(src, dst, send, recv, peer):
        copy = pltpu.make_async_remote_copy(
            src_ref=src, dst_ref=dst, send_sem=send, recv_sem=recv, device_id=peer, device_id_type=MESH
        )
        copy.start()
        sends.append(copy)

    def landed(ref, sem):
        pltpu.make_async_copy(ref, ref, sem).wait()

    sends = []
    pl.semaphore_wait(barrier, len(peers))

    lev = pl.ds(0, LEV)
    lev1 = pl.ds(1, LEV)
    (west, east) = beside
    left_side, right_side = 1 - first, last
    remote(q_a.at[lev1, pl.ds(5, 1)], near.at[lev, pl.ds(5, 1)], send1.at[0], recv1.at[0], east)
    remote(q_a.at[lev1, pl.ds(2, 1)], near.at[lev, pl.ds(2, 1)], send1.at[1], recv1.at[1], west)
    remote(packed.at[0], ext1.at[left_side], send1x.at[0], recv1x.at[left_side], left[0])
    remote(packed.at[0], ext1.at[right_side], send1x.at[1], recv1x.at[right_side], right[0])

    def send_packed(slot):
        for j in range(3):
            at = (0, 2, 1)[j]
            remote(packed.at[slot + 1], ext2.at[slot, left_side, at], send2x.at[slot, 0, j],
                   recv2x.at[slot, left_side, at], left[j])
            remote(packed.at[slot + 1], ext2.at[slot, right_side, at], send2x.at[slot, 1, j],
                   recv2x.at[slot, right_side, at], right[j])

    pack_field(d_in, 1, 0)
    loads[2].wait()
    pack_field(h_in, 2, 0)
    for slot, ref in ((0, d_in), (1, h_in)):
        remote(ref.at[lev, pl.ds(3, 3)], wide.at[slot, 0, lev, pl.ds(3, 3)], send2.at[slot, 0], recv2.at[slot, 0], east)
        remote(ref.at[lev, pl.ds(2, 3)], wide.at[slot, 1, lev, pl.ds(2, 3)], send2.at[slot, 1], recv2.at[slot, 1], west)
        send_packed(slot)

    for p in range(GROUPS):
        below = jnp.zeros((8, 128), F32)
        above = jnp.zeros((8, 128), F32)
        for i in range(GROUP):
            k = p * GROUP + i
            here = (lane >= 8 * i) & (lane < 8 * i + 8)
            below = jnp.where(here, couple[k + 1], below)
            above = jnp.where(here, couple[k], above)
        ey[1, p] = below
        ey[2, p] = above

    def mirrored(value, side):
        if side == 0:
            out = roll(value, -1, 2)
            for c, s in ((0, -7), (1, -5), (2, -3)):
                out = jnp.where(col5 == c, roll(value, s, 2), out)
            return jnp.where(jnp.full(value.shape, first, jnp.int32) == 1, out, value)
        out = roll(value, 1, 2)
        for c, s in ((5, 3), (6, 5), (7, 7)):
            out = jnp.where(col5 == c, roll(value, s, 2), out)
        return jnp.where(jnp.full(value.shape, last, jnp.int32) == 1, out, value)

    def both_sides(part):
        return jnp.where(col5 < 4, mirrored(part(0), 0), mirrored(part(1), 1))

    def ring_center(slot):
        def part(side):
            lo, hi = roll(ext2[slot, side, 1], 4, 1), roll(ext2[slot, side, 2], 4, 1)
            return jnp.where(sub5 < 2, lo, jnp.where(sub5 >= 6, hi, ext2[slot, side, 0]))

        return both_sides(part)

    def ring_outer(slot):
        def part(side):
            lo, hi = roll(ext2[slot, side, 1], 4, 1), roll(ext2[slot, side, 2], 4, 1)
            return jnp.where(sub5 < 2, hi, lo)

        return both_sides(part)

    def edges(value):
        return jnp.where(col5 == 3, roll(value, -1, 2), roll(value, 1, 2))

    def lat_sum(q, edge, i):
        e = roll(edge, 124 - 8 * i, 1)
        return jnp.where(lane == 0, e, roll(q, 1, 1)) + jnp.where(lane == 127, e, roll(q, -1, 1))

    def stencil(q, up, down, h4, lon_sum, lat, k):
        flux = couple[k + 1] * (q - down) - couple[k] * (up - q)
        return h4 * q - lon_sum - lat + flux

    landed(near.at[lev, pl.ds(5, 1)], recv1.at[0])
    landed(near.at[lev, pl.ds(2, 1)], recv1.at[1])
    landed(ext1.at[0], recv1x.at[0])
    landed(ext1.at[1], recv1x.at[1])
    ey[0] = edges(both_sides(lambda side: ext1[side]))
    loads[3].wait()

    def first_residual(p, acc):
        tile = jnp.zeros((8, 128), F32)
        edge = ey[0, p]
        for i in range(GROUP):
            k = p * GROUP + i
            q = q_a[k + 1]
            n = roll(near[k], 4, 0)
            lon_sum = roll(jnp.where(sub == 6, n, q), -1, 0) + roll(jnp.where(sub == 1, n, q), 1, 0)
            d = d_in[k]
            t = stencil(q, q_a[k], q_a[k + 2], 4.0 + h_in[k], lon_sum, lat_sum(q, edge, i), k)
            r = b_in[k] - d * t
            vs[0, k] = r
            acc = acc + r * r
            value = d * r
            q_b[k + 1] = value
            tile = pack_in(tile, value, i)
        packed[3, p] = tile
        return acc

    zero = jnp.zeros((8, 128), F32)
    moments = [levels(first_residual, zero)]

    remote(q_b.at[lev1, pl.ds(2, ROWS)], wide.at[2, 0, lev, pl.ds(2, ROWS)], send2.at[2, 0], recv2.at[2, 0], east)
    remote(q_b.at[lev1, pl.ds(2, ROWS)], wide.at[2, 1, lev, pl.ds(2, ROWS)], send2.at[2, 1], recv2.at[2, 1], west)
    send_packed(2)

    def wait_ring(slot):
        east_rows, west_rows = (pl.ds(3, 3), pl.ds(2, 3)) if slot < 2 else (pl.ds(2, ROWS),) * 2
        landed(wide.at[slot, 0, lev, east_rows], recv2.at[slot, 0])
        landed(wide.at[slot, 1, lev, west_rows], recv2.at[slot, 1])
        for side in range(2):
            for j in range(3):
                landed(ext2.at[slot, side, j], recv2x.at[slot, side, j])

    def gather(slot, ref, at, center, outer, center_at, plus):
        def step(p, _):
            for i in range(GROUP):
                k = p * GROUP + i
                w, e = roll(wide[slot, 0, k], 4, 0), roll(wide[slot, 1, k], 4, 0)
                mine = ref[k + at]
                center[k + center_at] = jnp.where(sub < 2, w, jnp.where(sub >= 6, e, mine)) + plus
                outer[k + center_at] = jnp.where(sub < 2, e, w) + plus
            return 0

        levels(step, 0)

    for slot, ref, center, outer, plus in ((0, d_in, d_c, d_o, 0.0), (1, h_in, h_c, h_o, 4.0)):
        wait_ring(slot)
        gather(slot, ref, 0, center, outer, 0, plus)
        ex[slot] = ring_center(slot) + plus
    wait_ring(2)
    gather(2, q_b, 1, q_c, o_a, 1, 0.0)
    ring = ring_center(2)
    ring_o = ring_outer(2)
    ey[0] = edges(ring)
    ey[3] = edges(ring_o)

    def ring_step(x, edge_tiles, outer):
        right_of = roll(jnp.where(col5 == 4, edge_tiles, x), -1, 2)
        left_of = roll(jnp.where(col5 == 3, edge_tiles, x), 1, 2)
        o = x if outer is None else outer
        lon_sum = roll(jnp.where(sub5 == 0, o, x), -1, 1) + roll(jnp.where(sub5 == 7, o, x), 1, 1)
        ahead, behind = roll(x, -8, 2), roll(x, 8, 2)
        none = jnp.zeros((1, 8, 128), F32)
        down = jnp.where(lane5 >= 120, jnp.concatenate([ahead[1:], none]), ahead)
        up = jnp.where(lane5 < 8, jnp.concatenate([none, behind[:-1]]), behind)
        t = ex[1] * x - lon_sum - (left_of + right_of) + (ey[1] * (x - down) - ey[2] * (up - x))
        d = ex[0]
        return d * (d * t)

    def apply(n, src, dst, out_src, out_dst, slot):
        def step(p, acc):
            even, odd = acc
            tile = jnp.zeros((8, 128), F32)
            edge = ey[0, p]
            edge_o = ey[3, p]
            for i in range(GROUP):
                k = p * GROUP + i
                q = src[k + 1]
                o = q if out_src is None else out_src[k + 1]
                lon_sum = roll(jnp.where(sub == 0, o, q), -1, 0) + roll(jnp.where(sub == 7, o, q), 1, 0)
                d = d_c[k]
                v = d * stencil(q, src[k], src[k + 2], h_c[k], lon_sum, lat_sum(q, edge, i), k)
                vs[n, k] = v
                odd = odd + vs[n - 1, k] * v
                even = even + v * v
                if dst is not None:
                    value = d * v
                    dst[k + 1] = value
                    tile = pack_in(tile, value, i)
                if out_dst is not None:
                    lon_o = roll(jnp.where(sub == 0, q, o), -1, 0) + roll(jnp.where(sub == 7, q, o), 1, 0)
                    do = d_o[k]
                    to = stencil(o, out_src[k], out_src[k + 2], h_o[k], lon_o, lat_sum(o, edge_o, i), k)
                    out_dst[k + 1] = do * (do * to)
            if dst is not None:
                ex[slot, p] = tile
            return even, odd

        even, odd = levels(step, (zero, zero))
        moments.extend([odd, even])

    def pack_ref(ref, slot):
        def step(p, _):
            tile = jnp.zeros((8, 128), F32)
            for i in range(GROUP):
                tile = pack_in(tile, ref[p * GROUP + i + 1], i)
            ex[slot, p] = tile
            return 0

        levels(step, 0)

    pack_ref(q_c, 2)
    apply(1, q_c, q_d, o_a, o_b, 3)
    ring = ring_step(ring, ex[2], ring_o)
    ey[0] = edges(ring)
    apply(2, q_d, q_c, o_b, None, 2)
    ring = ring_step(ring, ex[3], None)
    ey[0] = edges(ring)
    apply(3, q_c, q_d, None, None, 3)
    ring = ring_step(ring, ex[2], None)
    ey[0] = edges(ring)
    apply(4, q_d, None, None, None, 2)

    def total(acc):
        value = jnp.where(is_own, acc, 0.0)
        pair = two_sum(value, roll(value, -2, 0))
        return dd_add(pair, tuple(roll(part, -1, 0) for part in pair))

    pairs = [total(acc) for acc in moments]
    row = jnp.zeros((8, 128), F32)
    for start in (0, 8):
        high, low = zero, zero
        for k in range(start, min(start + 8, len(pairs))):
            shift = k - start - 2
            high = jnp.where(sub == k - start, roll(pairs[k][0], shift, 0), high)
            low = jnp.where(sub == k - start, roll(pairs[k][1], shift, 0), low)
        pair = (high, low)
        for width in (64, 32, 16, 8, 4, 2, 1):
            pair = dd_add(pair, tuple(roll(part, width, 1) for part in pair))
        row = row + jnp.where(lane == sub + start, pair[0], 0.0) + jnp.where(lane == sub + start + 16, pair[1], 0.0)
    for width in (4, 2, 1):
        row = row + roll(row, width, 0)

    def sum_over(row, line, slots, me, group, size, send, recv):
        line[...] = row
        slots[pl.ds(me, 1), :] = row[0:1]
        for peer in group:
            copy = pltpu.make_async_remote_copy(
                src_ref=line.at[pl.ds(0, 1)], dst_ref=slots.at[pl.ds(me, 1)], send_sem=send.at[0],
                recv_sem=recv.at[0], device_id=peer, device_id_type=MESH,
            )
            copy.start()
        landed(slots.at[pl.ds(0, size - 1)], recv.at[0])
        parts = [(slots[8 * j : 8 * j + 8], zero) for j in range(size // 8)]
        while len(parts) > 1:
            parts = [
                dd_add_raw(parts[j], parts[j + 1]) if j + 1 < len(parts) else parts[j] for j in range(0, len(parts), 2)
            ]
        pair = parts[0]
        for width in (4, 2, 1):
            pair = dd_add_raw(pair, tuple(roll(part, width, 0) for part in pair))
        low = pair[1] + roll(pair[0], -16, 1)
        high, low = quick_two_sum(pair[0], low)
        return jnp.where(lane < 16, high, jnp.where(lane < 32, roll(low, 16, 1), 0.0))

    def dd_add_raw(a, b):
        s, e = two_sum(a[0], b[0])
        return s, e + (a[1] + b[1])

    row = sum_over(row, row_a, sums_a, me_a, group_a, SIZE_A, send_a, recv_a)
    row = sum_over(row, row_b, sums_b, me_b, group_b, SIZE_B, send_b, recv_b)

    m = (row, roll(row, -16, 1))

    def at(pair, k):
        return tuple(jnp.broadcast_to(part[:, k : k + 1], (8, 128)) for part in pair)

    def ahead(pair, k):
        return tuple(roll(part, -k, 1) for part in pair)

    one = (jnp.ones((8, 128), F32), zero)
    m0, m1, m2, m3 = (at(m, k) for k in range(4))
    alpha = dd_div(m0, m1)
    g = dd_sub(m, dd_mul(alpha, ahead(m, 1)))
    t = dd_sub(g, dd_mul(alpha, ahead(g, 1)))
    omega = dd_div(at(t, 1), at(t, 2))
    rho = dd_sub(at(g, 0), dd_mul(omega, at(g, 1)))
    beta = dd_mul(dd_div(rho, m0), dd_div(alpha, omega))
    both = dd_add(alpha, omega)
    d0 = dd_add(one, beta)
    d1 = dd_neg(dd_add(both, dd_mul(beta, omega)))
    d2 = dd_mul(alpha, omega)
    image = dd_add(dd_add(dd_mul(d0, m1), dd_mul(d1, m2)), dd_mul(d2, m3))
    alpha1 = dd_div(rho, image)
    h1 = dd_neg(dd_add(both, dd_mul(alpha1, d0)))
    h2 = dd_sub(d2, dd_mul(alpha1, d1))
    h3 = dd_neg(dd_mul(alpha1, d2))

    def half_with(pair):
        out = pair
        for j, h in ((1, h1), (2, h2), (3, h3)):
            out = dd_add(out, dd_mul(h, ahead(pair, j)))
        return out

    t = half_with(half_with(m))
    omega1 = dd_div(at(t, 1), at(t, 2))
    res_c = (
        one,
        dd_sub(h1, omega1),
        dd_sub(h2, dd_mul(omega1, h1)),
        dd_sub(h3, dd_mul(omega1, h2)),
        dd_neg(dd_mul(omega1, h3)),
    )
    sol_c = (
        dd_add(dd_add(both, dd_mul(alpha1, d0)), omega1),
        dd_add(dd_sub(dd_mul(alpha1, d1), d2), dd_mul(omega1, h1)),
        dd_add(dd_mul(alpha1, d2), dd_mul(omega1, h2)),
        dd_mul(omega1, h3),
    )

    def finish(p, _):
        for i in range(GROUP):
            k = p * GROUP + i
            v = [vs[n, k] for n in range(5)]
            sol[k] = x_in[k] + (sol_c[0][0] * v[0] + sol_c[1][0] * v[1] + sol_c[2][0] * v[2] + sol_c[3][0] * v[3])
            res[k] = v[0] + (res_c[1][0] * v[1] + res_c[2][0] * v[2] + res_c[3][0] * v[3] + res_c[4][0] * v[4])
        return 0

    levels(finish, 0)
    stores = [
        pltpu.make_async_copy(src.at[lev, pl.ds(2, ROWS)], dst, load_sem.at[i])
        for i, (src, dst) in enumerate(((sol, sol_hbm), (res, res_hbm)))
    ]
    for copy in stores:
        copy.start()
    for copy in sends:
        copy.wait_send()
    landed(sums_a.at[pl.ds(0, SIZE_A - 1)], send_a.at[0])
    landed(sums_b.at[pl.ds(0, SIZE_B - 1)], send_b.at[0])
    for copy in stores:
        copy.wait()


def body(right_side, first_guess, cell_scale, helmholtz_term, vertical_coupling):
    block = jax.ShapeDtypeStruct((LEV, ROWS, 128), F32)
    field = pltpu.VMEM((PAD, 8, 128), F32)
    guarded = pltpu.VMEM((PAD + 2, 8, 128), F32)
    dma = pltpu.SemaphoreType.DMA
    return pl.pallas_call(
        kernel,
        out_shape=(block, block),
        in_specs=[pl.BlockSpec(memory_space=pl.ANY)] * 4 + [pl.BlockSpec(memory_space=pltpu.SMEM)],
        out_specs=(pl.BlockSpec(memory_space=pl.ANY),) * 2,
        scratch_shapes=[
            *[field] * 8,
            *[guarded] * 6,
            field,
            pltpu.VMEM((3, 2, PAD, 8, 128), F32),
            pltpu.VMEM((5, PAD, 8, 128), F32),
            pltpu.VMEM((4, GROUPS, 8, 128), F32),
            pltpu.VMEM((2, GROUPS, 8, 128), F32),
            pltpu.VMEM((3, 2, 3, GROUPS, 8, 128), F32),
            pltpu.VMEM((4, GROUPS, 8, 128), F32),
            pltpu.VMEM((4, GROUPS, 8, 128), F32),
            pltpu.VMEM((SIZE_A, 128), F32),
            pltpu.VMEM((SIZE_B, 128), F32),
            pltpu.VMEM((8, 128), F32),
            pltpu.VMEM((8, 128), F32),
            pltpu.SMEM((PAD + 2,), F32),
            field,
            field,
            dma((4,)),
            dma((2,)),
            dma((2,)),
            dma((2,)),
            dma((2,)),
            dma((3, 2)),
            dma((3, 2)),
            dma((3, 2, 3)),
            dma((3, 2, 3)),
            *[dma((1,))] * 4,
        ],
        compiler_params=pltpu.CompilerParams(collective_id=0, has_side_effects=True, vmem_limit_bytes=48 << 20),
        cost_estimate=pl.CostEstimate(flops=8_000_000, bytes_accessed=900_000, transcendentals=0),
    )(right_side, first_guess, cell_scale, helmholtz_term, vertical_coupling)


def solution(mesh):
    spec = P(None, "lon", "lat")
    return jax.shard_map(
        body, mesh=mesh, in_specs=(spec, spec, spec, spec, P()), out_specs=(spec, spec), check_vma=False
    )
```

```python
import jax
import jax.numpy as jnp
from jax import lax
from jax.experimental import pallas as pl
from jax.experimental.pallas import tpu as pltpu
from jax.sharding import PartitionSpec as P

MESH = pl.DeviceIdType.MESH
F32 = jnp.float32

LEV = 70
GROUP = 16
GROUPS = 5
PAD = GROUP * GROUPS
ROWS = 4
NX, NYH, NZ, NYL, NC = 4, 2, 12, 4, 2
NLONB, NBAND = NX * NYH * NZ, NYL * NC
SIZE_A, SIZE_B = NX * NYH * NYL, NZ * NC


def two_sum(a, b):
    s = a + b
    t = s - a
    return s, (a - (s - t)) + (b - t)


def quick_two_sum(a, b):
    s = a + b
    return s, b - (s - a)


def split(a):
    c = 4097.0 * a
    high = c - (c - a)
    return high, a - high


def two_prod(a, b):
    p = a * b
    ah, al = split(a)
    bh, bl = split(b)
    return p, ((ah * bh - p) + ah * bl + al * bh) + al * bl


def dd_add(a, b):
    s, e = two_sum(a[0], b[0])
    return quick_two_sum(s, e + (a[1] + b[1]))


def dd_neg(a):
    return -a[0], -a[1]


def dd_sub(a, b):
    return dd_add(a, dd_neg(b))


def dd_mul(a, b):
    p, e = two_prod(a[0], b[0])
    return quick_two_sum(p, e + (a[0] * b[1] + a[1] * b[0]))


def dd_div(a, b):
    q = a[0] / b[0]
    zero = jnp.zeros_like(q)
    r = dd_sub(a, dd_mul((q, zero), b))
    return quick_two_sum(q, r[0] / b[0])


def roll(x, shift, axis):
    return pltpu.roll(x, shift % x.shape[axis], axis)


def halo_peers():
    lon, band = lax.axis_index("lon"), lax.axis_index("lat")
    west, east = lax.rem(lon + NLONB - 1, NLONB), lax.rem(lon + 1, NLONB)
    first = 1 - jnp.minimum(band, 1)
    last = jnp.maximum(band, NBAND - 2) - (NBAND - 2)

    def across(index, pole):
        return lax.rem(index + pole * (NLONB // 2), NLONB)

    left_band, right_band = band - 1 + first, band + 1 - last
    beside = ((west, band), (east, band))
    left = tuple((across(i, first), left_band) for i in (lon, west, east))
    right = tuple((across(i, last), right_band) for i in (lon, west, east))
    return beside, left, right, first, last


def sum_peers():
    lon, band = lax.axis_index("lon"), lax.axis_index("lat")
    x, y_hi, z = lax.rem(lon, NX), lax.rem(lon // NX, NYH), lon // (NX * NYH)
    core, y_lo = lax.rem(band, NC), band // NC
    me_a = (y_hi * NYL + y_lo) * NX + x
    me_b = z * NC + core
    group_a, group_b = [], []
    for j in range(1, SIZE_A):
        t = lax.rem(me_a + j, SIZE_A)
        px, py = lax.rem(t, NX), t // NX
        group_a.append(((z * NYH + py // NYL) * NX + px, lax.rem(py, NYL) * NC + core))
    for j in range(1, SIZE_B):
        t = lax.rem(me_b + j, SIZE_B)
        pc, pz = lax.rem(t, NC), t // NC
        group_b.append(((pz * NYH + y_hi) * NX + x, y_lo * NC + pc))
    return (me_a, group_a), (me_b, group_b)


def kernel(
    b_hbm, x_hbm, d_hbm, h_hbm, vc_hbm, sol_hbm, res_hbm,
    b_in, x_in, d_in, h_in, d_c, h_c, d_o, h_o,
    q_a, q_b, q_c, q_d, o_a, o_b,
    near, wide, vs, packed, ext1, ext2, ex, ey, sums_a, sums_b, row_a, row_b, vc, couple, sol, res,
    load_sem, send1, recv1, send1x, recv1x, send2, recv2, send2x, recv2x, send_a, recv_a, send_b, recv_b,
):
    beside, left, right, first, last = halo_peers()
    (me_a, group_a), (me_b, group_b) = sum_peers()

    loads = [
        pltpu.make_async_copy(src, dst.at[pl.ds(0, LEV), pl.ds(2, ROWS)], load_sem.at[i])
        for i, (src, dst) in enumerate(((d_hbm, d_in), (x_hbm, x_in), (h_hbm, h_in), (b_hbm, b_in)))
    ]
    loads.append(pltpu.make_async_copy(vc_hbm, vc, load_sem.at[4]))
    for copy in loads:
        copy.start()

    barrier = pltpu.get_barrier_semaphore()
    peers = [*beside, *left, *right, *group_a, *group_b]
    for peer in peers:
        pl.semaphore_signal(barrier, inc=1, device_id=peer, device_id_type=MESH)

    lane = lax.broadcasted_iota(jnp.int32, (8, 128), 1)
    sub = lax.broadcasted_iota(jnp.int32, (8, 128), 0)
    lane5 = lax.broadcasted_iota(jnp.int32, (GROUPS, 8, 128), 2)
    sub5 = lax.broadcasted_iota(jnp.int32, (GROUPS, 8, 128), 1)
    col5 = lax.rem(lane5, 8)
    lane8 = lane // 8
    is_own = (sub >= 2) & (sub < 6)

    tail = jnp.zeros((PAD - LEV, 8, 128), F32)
    for ref in (b_in, x_in, d_in, h_in, near):
        ref[LEV:PAD] = tail
    for i in range(3):
        for j in range(2):
            wide[i, j, LEV:PAD] = tail
    for ref in (q_a, q_b, q_c, q_d, o_a, o_b):
        ref[0] = jnp.zeros((8, 128), F32)
        ref[PAD + 1] = jnp.zeros((8, 128), F32)

    def levels(step, init):
        def group(p, carry):
            return step(p, carry)

        return lax.fori_loop(0, GROUPS, group, init)

    def pack_in(tile, value, i):
        return jnp.where(lane8 == i, roll(value, 8 * i + 4, 1), tile)

    def pack_field(ref, slot, at):
        def step(p, _):
            tile = jnp.zeros((8, 128), F32)
            for i in range(GROUP):
                tile = pack_in(tile, ref[p * GROUP + i + at], i)
            packed[slot, p] = tile
            return 0

        levels(step, 0)

    loads[0].wait()
    loads[1].wait()

    def scaled_guess(p, _):
        tile = jnp.zeros((8, 128), F32)
        for i in range(GROUP):
            k = p * GROUP + i
            value = d_in[k] * x_in[k]
            q_a[k + 1] = value
            tile = pack_in(tile, value, i)
        packed[0, p] = tile
        return 0

    levels(scaled_guess, 0)

    def remote(src, dst, send, recv, peer):
        copy = pltpu.make_async_remote_copy(
            src_ref=src, dst_ref=dst, send_sem=send, recv_sem=recv, device_id=peer, device_id_type=MESH
        )
        copy.start()
        sends.append(copy)

    def landed(ref, sem):
        pltpu.make_async_copy(ref, ref, sem).wait()

    sends = []
    pl.semaphore_wait(barrier, len(peers))

    lev = pl.ds(0, LEV)
    lev1 = pl.ds(1, LEV)
    (west, east) = beside
    left_side, right_side = 1 - first, last
    remote(q_a.at[lev1, pl.ds(5, 1)], near.at[lev, pl.ds(5, 1)], send1.at[0], recv1.at[0], east)
    remote(q_a.at[lev1, pl.ds(2, 1)], near.at[lev, pl.ds(2, 1)], send1.at[1], recv1.at[1], west)
    mine = (slice(None), pl.ds(2, ROWS))
    remote(packed.at[0, *mine], ext1.at[left_side, *mine], send1x.at[0], recv1x.at[left_side], left[0])
    remote(packed.at[0, *mine], ext1.at[right_side, *mine], send1x.at[1], recv1x.at[right_side], right[0])

    def ring_rows(slot, at):
        deep = 2 if slot < 2 else 3
        return slice(None), (pl.ds(2, ROWS), pl.ds(6 - deep, deep), pl.ds(2, deep))[at]

    def send_packed(slot):
        for j in (1, 2, 0):
            at = (0, 2, 1)[j]
            rows = ring_rows(slot, at)
            remote(packed.at[slot + 1, *rows], ext2.at[slot, left_side, at, *rows], send2x.at[slot, 0, j],
                   recv2x.at[slot, left_side, at], left[j])
            remote(packed.at[slot + 1, *rows], ext2.at[slot, right_side, at, *rows], send2x.at[slot, 1, j],
                   recv2x.at[slot, right_side, at], right[j])

    loads[2].wait()
    for slot, ref in ((0, d_in), (1, h_in)):
        remote(ref.at[lev, pl.ds(3, 3)], wide.at[slot, 0, lev, pl.ds(3, 3)], send2.at[slot, 0], recv2.at[slot, 0], east)
        remote(ref.at[lev, pl.ds(2, 3)], wide.at[slot, 1, lev, pl.ds(2, 3)], send2.at[slot, 1], recv2.at[slot, 1], west)
    for slot, ref in ((0, d_in), (1, h_in)):
        pack_field(ref, slot + 1, 0)
        send_packed(slot)

    loads[4].wait()
    for k in range(PAD + 2):
        couple[k] = vc[k - 1] if 1 <= k < LEV else jnp.float32(0.0)

    for p in range(GROUPS):
        below = jnp.zeros((8, 128), F32)
        above = jnp.zeros((8, 128), F32)
        for i in range(GROUP):
            k = p * GROUP + i
            here = lane8 == i
            below = jnp.where(here, couple[k + 1], below)
            above = jnp.where(here, couple[k], above)
        ey[1, p] = below
        ey[2, p] = above

    def mirrored(value, side):
        if side == 0:
            out = roll(value, -1, 2)
            for c, s in ((0, -7), (1, -5), (2, -3)):
                out = jnp.where(col5 == c, roll(value, s, 2), out)
            return jnp.where(jnp.full(value.shape, first, jnp.int32) == 1, out, value)
        out = roll(value, 1, 2)
        for c, s in ((5, 3), (6, 5), (7, 7)):
            out = jnp.where(col5 == c, roll(value, s, 2), out)
        return jnp.where(jnp.full(value.shape, last, jnp.int32) == 1, out, value)

    def both_sides(part):
        return jnp.where(col5 < 4, mirrored(part(0), 0), mirrored(part(1), 1))

    def ring_center(slot):
        def part(side):
            lo, hi = roll(ext2[slot, side, 1], 4, 1), roll(ext2[slot, side, 2], 4, 1)
            return jnp.where(sub5 < 2, lo, jnp.where(sub5 >= 6, hi, ext2[slot, side, 0]))

        return both_sides(part)

    def ring_outer(slot):
        def part(side):
            lo, hi = roll(ext2[slot, side, 1], 4, 1), roll(ext2[slot, side, 2], 4, 1)
            return jnp.where(sub5 < 2, hi, lo)

        return both_sides(part)

    def edges(value):
        return jnp.where(col5 == 3, roll(value, -1, 2), roll(value, 1, 2))

    def lat_sum(q, edge, i):
        e = roll(edge, 124 - 8 * i, 1)
        return jnp.where(lane == 0, e, roll(q, 1, 1)) + jnp.where(lane == 127, e, roll(q, -1, 1))

    def stencil(q, up, down, h4, lon_sum, lat, k):
        flux = couple[k + 1] * (q - down) - couple[k] * (up - q)
        return h4 * q - lon_sum - lat + flux

    landed(near.at[lev, pl.ds(5, 1)], recv1.at[0])
    landed(near.at[lev, pl.ds(2, 1)], recv1.at[1])
    landed(ext1.at[0, *mine], recv1x.at[0])
    landed(ext1.at[1, *mine], recv1x.at[1])
    ey[0] = edges(both_sides(lambda side: ext1[side]))
    loads[3].wait()

    def first_residual(p, acc):
        tile = jnp.zeros((8, 128), F32)
        edge = ey[0, p]
        for i in range(GROUP):
            k = p * GROUP + i
            q = q_a[k + 1]
            n = roll(near[k], 4, 0)
            lon_sum = roll(jnp.where(sub == 6, n, q), -1, 0) + roll(jnp.where(sub == 1, n, q), 1, 0)
            d = d_in[k]
            t = stencil(q, q_a[k], q_a[k + 2], 4.0 + h_in[k], lon_sum, lat_sum(q, edge, i), k)
            r = b_in[k] - d * t
            vs[0, k] = r
            acc = acc + r * r
            value = d * r
            q_b[k + 1] = value
            tile = pack_in(tile, value, i)
        packed[3, p] = tile
        return acc

    zero = jnp.zeros((8, 128), F32)
    moments = [levels(first_residual, zero)]

    send_packed(2)
    remote(q_b.at[lev1, pl.ds(2, ROWS)], wide.at[2, 0, lev, pl.ds(2, ROWS)], send2.at[2, 0], recv2.at[2, 0], east)
    remote(q_b.at[lev1, pl.ds(2, ROWS)], wide.at[2, 1, lev, pl.ds(2, ROWS)], send2.at[2, 1], recv2.at[2, 1], west)

    def wait_ring(slot):
        east_rows, west_rows = (pl.ds(3, 3), pl.ds(2, 3)) if slot < 2 else (pl.ds(2, ROWS),) * 2
        landed(wide.at[slot, 0, lev, east_rows], recv2.at[slot, 0])
        landed(wide.at[slot, 1, lev, west_rows], recv2.at[slot, 1])
        for side in range(2):
            for j in range(3):
                landed(ext2.at[slot, side, j, *ring_rows(slot, j)], recv2x.at[slot, side, j])

    def gather(slot, ref, at, center, outer, center_at, plus):
        def step(p, _):
            for i in range(GROUP):
                k = p * GROUP + i
                w, e = roll(wide[slot, 0, k], 4, 0), roll(wide[slot, 1, k], 4, 0)
                mine = ref[k + at]
                center[k + center_at] = jnp.where(sub < 2, w, jnp.where(sub >= 6, e, mine)) + plus
                outer[k + center_at] = jnp.where(sub < 2, e, w) + plus
            return 0

        levels(step, 0)

    for slot, ref, center, outer, plus in ((0, d_in, d_c, d_o, 0.0), (1, h_in, h_c, h_o, 4.0)):
        wait_ring(slot)
        gather(slot, ref, 0, center, outer, 0, plus)
        ex[slot] = ring_center(slot) + plus
    wait_ring(2)
    gather(2, q_b, 1, q_c, o_a, 1, 0.0)
    ring = ring_center(2)
    ring_o = ring_outer(2)
    ey[0] = edges(ring)
    ey[3] = edges(ring_o)

    def ring_step(x, edge_tiles, outer):
        right_of = roll(jnp.where(col5 == 4, edge_tiles, x), -1, 2)
        left_of = roll(jnp.where(col5 == 3, edge_tiles, x), 1, 2)
        o = x if outer is None else outer
        lon_sum = roll(jnp.where(sub5 == 0, o, x), -1, 1) + roll(jnp.where(sub5 == 7, o, x), 1, 1)
        ahead, behind = roll(x, -8, 2), roll(x, 8, 2)
        none = jnp.zeros((1, 8, 128), F32)
        down = jnp.where(lane5 >= 120, jnp.concatenate([ahead[1:], none]), ahead)
        up = jnp.where(lane5 < 8, jnp.concatenate([none, behind[:-1]]), behind)
        t = ex[1] * x - lon_sum - (left_of + right_of) + (ey[1] * (x - down) - ey[2] * (up - x))
        d = ex[0]
        return d * (d * t)

    def apply(n, src, dst, out_src, out_dst, slot):
        def step(p, acc):
            even, odd = acc
            tile = jnp.zeros((8, 128), F32)
            edge = ey[0, p]
            edge_o = ey[3, p]
            for i in range(GROUP):
                k = p * GROUP + i
                q = src[k + 1]
                o = q if out_src is None else out_src[k + 1]
                lon_sum = roll(jnp.where(sub == 0, o, q), -1, 0) + roll(jnp.where(sub == 7, o, q), 1, 0)
                d = d_c[k]
                v = d * stencil(q, src[k], src[k + 2], h_c[k], lon_sum, lat_sum(q, edge, i), k)
                vs[n, k] = v
                odd = odd + vs[n - 1, k] * v
                even = even + v * v
                if dst is not None:
                    value = d * v
                    dst[k + 1] = value
                    tile = pack_in(tile, value, i)
                if out_dst is not None:
                    lon_o = roll(jnp.where(sub == 0, q, o), -1, 0) + roll(jnp.where(sub == 7, q, o), 1, 0)
                    do = d_o[k]
                    to = stencil(o, out_src[k], out_src[k + 2], h_o[k], lon_o, lat_sum(o, edge_o, i), k)
                    out_dst[k + 1] = do * (do * to)
            if dst is not None:
                ex[slot, p] = tile
            return even, odd

        even, odd = levels(step, (zero, zero))
        moments.extend([odd, even])

    def pack_ref(ref, slot):
        def step(p, _):
            tile = jnp.zeros((8, 128), F32)
            for i in range(GROUP):
                tile = pack_in(tile, ref[p * GROUP + i + 1], i)
            ex[slot, p] = tile
            return 0

        levels(step, 0)

    pack_ref(q_c, 2)
    apply(1, q_c, q_d, o_a, o_b, 3)
    ring = ring_step(ring, ex[2], ring_o)
    ey[0] = edges(ring)
    apply(2, q_d, q_c, o_b, None, 2)
    ring = ring_step(ring, ex[3], None)
    ey[0] = edges(ring)
    apply(3, q_c, q_d, None, None, 3)
    ring = ring_step(ring, ex[2], None)
    ey[0] = edges(ring)
    apply(4, q_d, None, None, None, 2)

    def total(acc):
        value = jnp.where(is_own, acc, 0.0)
        pair = two_sum(value, roll(value, -2, 0))
        return dd_add(pair, tuple(roll(part, -1, 0) for part in pair))

    pairs = [total(acc) for acc in moments]
    row = jnp.zeros((8, 128), F32)
    for start in (0, 8):
        high, low = zero, zero
        for k in range(start, min(start + 8, len(pairs))):
            shift = k - start - 2
            high = jnp.where(sub == k - start, roll(pairs[k][0], shift, 0), high)
            low = jnp.where(sub == k - start, roll(pairs[k][1], shift, 0), low)
        pair = (high, low)
        for width in (64, 32, 16, 8, 4, 2, 1):
            pair = dd_add(pair, tuple(roll(part, width, 1) for part in pair))
        row = row + jnp.where(lane == sub + start, pair[0], 0.0) + jnp.where(lane == sub + start + 16, pair[1], 0.0)
    for width in (4, 2, 1):
        row = row + roll(row, width, 0)

    def sum_over(row, line, slots, me, group, size, send, recv):
        line[...] = row
        slots[pl.ds(me, 1), :] = row[0:1]
        for peer in group:
            copy = pltpu.make_async_remote_copy(
                src_ref=line.at[pl.ds(0, 1)], dst_ref=slots.at[pl.ds(me, 1)], send_sem=send.at[0],
                recv_sem=recv.at[0], device_id=peer, device_id_type=MESH,
            )
            copy.start()
        landed(slots.at[pl.ds(0, size - 1)], recv.at[0])
        parts = [(slots[8 * j : 8 * j + 8], zero) for j in range(size // 8)]
        while len(parts) > 1:
            parts = [
                dd_add_raw(parts[j], parts[j + 1]) if j + 1 < len(parts) else parts[j] for j in range(0, len(parts), 2)
            ]
        pair = parts[0]
        for width in (4, 2, 1):
            pair = dd_add_raw(pair, tuple(roll(part, width, 0) for part in pair))
        low = pair[1] + roll(pair[0], -16, 1)
        high, low = quick_two_sum(pair[0], low)
        return jnp.where(lane < 16, high, jnp.where(lane < 32, roll(low, 16, 1), 0.0))

    def dd_add_raw(a, b):
        s, e = two_sum(a[0], b[0])
        return s, e + (a[1] + b[1])

    row = sum_over(row, row_a, sums_a, me_a, group_a, SIZE_A, send_a, recv_a)
    row = sum_over(row, row_b, sums_b, me_b, group_b, SIZE_B, send_b, recv_b)

    m = (row, roll(row, -16, 1))

    def at(pair, k):
        return tuple(jnp.broadcast_to(part[:, k : k + 1], (8, 128)) for part in pair)

    def ahead(pair, k):
        return tuple(roll(part, -k, 1) for part in pair)

    one = (jnp.ones((8, 128), F32), zero)
    m0, m1, m2, m3 = (at(m, k) for k in range(4))
    alpha = dd_div(m0, m1)
    g = dd_sub(m, dd_mul(alpha, ahead(m, 1)))
    t = dd_sub(g, dd_mul(alpha, ahead(g, 1)))
    omega = dd_div(at(t, 1), at(t, 2))
    rho = dd_sub(at(g, 0), dd_mul(omega, at(g, 1)))
    beta = dd_mul(dd_div(rho, m0), dd_div(alpha, omega))
    both = dd_add(alpha, omega)
    d0 = dd_add(one, beta)
    d1 = dd_neg(dd_add(both, dd_mul(beta, omega)))
    d2 = dd_mul(alpha, omega)
    image = dd_add(dd_add(dd_mul(d0, m1), dd_mul(d1, m2)), dd_mul(d2, m3))
    alpha1 = dd_div(rho, image)
    h1 = dd_neg(dd_add(both, dd_mul(alpha1, d0)))
    h2 = dd_sub(d2, dd_mul(alpha1, d1))
    h3 = dd_neg(dd_mul(alpha1, d2))

    def half_with(pair):
        out = pair
        for j, h in ((1, h1), (2, h2), (3, h3)):
            out = dd_add(out, dd_mul(h, ahead(pair, j)))
        return out

    t = half_with(half_with(m))
    omega1 = dd_div(at(t, 1), at(t, 2))
    res_c = (
        one,
        dd_sub(h1, omega1),
        dd_sub(h2, dd_mul(omega1, h1)),
        dd_sub(h3, dd_mul(omega1, h2)),
        dd_neg(dd_mul(omega1, h3)),
    )
    sol_c = (
        dd_add(dd_add(both, dd_mul(alpha1, d0)), omega1),
        dd_add(dd_sub(dd_mul(alpha1, d1), d2), dd_mul(omega1, h1)),
        dd_add(dd_mul(alpha1, d2), dd_mul(omega1, h2)),
        dd_mul(omega1, h3),
    )

    def finish(p, _):
        for i in range(GROUP):
            k = p * GROUP + i
            v = [vs[n, k] for n in range(5)]
            sol[k] = x_in[k] + (sol_c[0][0] * v[0] + sol_c[1][0] * v[1] + sol_c[2][0] * v[2] + sol_c[3][0] * v[3])
            res[k] = v[0] + (res_c[1][0] * v[1] + res_c[2][0] * v[2] + res_c[3][0] * v[3] + res_c[4][0] * v[4])
        return 0

    levels(finish, 0)
    stores = [
        pltpu.make_async_copy(src.at[lev, pl.ds(2, ROWS)], dst, load_sem.at[i])
        for i, (src, dst) in enumerate(((sol, sol_hbm), (res, res_hbm)))
    ]
    for copy in stores:
        copy.start()
    for copy in sends:
        copy.wait_send()
    landed(sums_a.at[pl.ds(0, SIZE_A - 1)], send_a.at[0])
    landed(sums_b.at[pl.ds(0, SIZE_B - 1)], send_b.at[0])
    for copy in stores:
        copy.wait()


def body(right_side, first_guess, cell_scale, helmholtz_term, vertical_coupling):
    block = jax.ShapeDtypeStruct((LEV, ROWS, 128), F32)
    field = pltpu.VMEM((PAD, 8, 128), F32)
    guarded = pltpu.VMEM((PAD + 2, 8, 128), F32)
    dma = pltpu.SemaphoreType.DMA
    return pl.pallas_call(
        kernel,
        out_shape=(block, block),
        in_specs=[pl.BlockSpec(memory_space=pl.ANY)] * 5,
        out_specs=(pl.BlockSpec(memory_space=pl.ANY),) * 2,
        scratch_shapes=[
            *[field] * 8,
            *[guarded] * 6,
            field,
            pltpu.VMEM((3, 2, PAD, 8, 128), F32),
            pltpu.VMEM((5, PAD, 8, 128), F32),
            pltpu.VMEM((4, GROUPS, 8, 128), F32),
            pltpu.VMEM((2, GROUPS, 8, 128), F32),
            pltpu.VMEM((3, 2, 3, GROUPS, 8, 128), F32),
            pltpu.VMEM((4, GROUPS, 8, 128), F32),
            pltpu.VMEM((4, GROUPS, 8, 128), F32),
            pltpu.VMEM((SIZE_A, 128), F32),
            pltpu.VMEM((SIZE_B, 128), F32),
            pltpu.VMEM((8, 128), F32),
            pltpu.VMEM((8, 128), F32),
            pltpu.SMEM((LEV - 1,), F32),
            pltpu.SMEM((PAD + 2,), F32),
            field,
            field,
            dma((5,)),
            dma((2,)),
            dma((2,)),
            dma((2,)),
            dma((2,)),
            dma((3, 2)),
            dma((3, 2)),
            dma((3, 2, 3)),
            dma((3, 2, 3)),
            *[dma((1,))] * 4,
        ],
        compiler_params=pltpu.CompilerParams(collective_id=0, has_side_effects=True, vmem_limit_bytes=60 << 20),
        cost_estimate=pl.CostEstimate(flops=8_000_000, bytes_accessed=900_000, transcendentals=0),
    )(right_side, first_guess, cell_scale, helmholtz_term, vertical_coupling)


def solution(mesh):
    spec = P(None, "lon", "lat")
    return jax.shard_map(
        body, mesh=mesh, in_specs=(spec, spec, spec, spec, P()), out_specs=(spec, spec), check_vma=False
    )
```

```python
import jax
import jax.numpy as jnp
from jax import lax
from jax.experimental import pallas as pl
from jax.experimental.pallas import tpu as pltpu
from jax.sharding import PartitionSpec as P

MESH = pl.DeviceIdType.MESH
F32 = jnp.float32

LEV = 70
GROUP = 16
GROUPS = 5
PAD = GROUP * GROUPS
ROWS = 4
NX, NYH, NZ, NYL, NC = 4, 2, 12, 4, 2
NLONB, NBAND = NX * NYH * NZ, NYL * NC
SIZE_A, SIZE_B = NX * NYH * NYL, NZ * NC


def two_sum(a, b):
    s = a + b
    t = s - a
    return s, (a - (s - t)) + (b - t)


def quick_two_sum(a, b):
    s = a + b
    return s, b - (s - a)


def split(a):
    c = 4097.0 * a
    high = c - (c - a)
    return high, a - high


def two_prod(a, b):
    p = a * b
    ah, al = split(a)
    bh, bl = split(b)
    return p, ((ah * bh - p) + ah * bl + al * bh) + al * bl


def dd_add(a, b):
    s, e = two_sum(a[0], b[0])
    return quick_two_sum(s, e + (a[1] + b[1]))


def dd_neg(a):
    return -a[0], -a[1]


def dd_sub(a, b):
    return dd_add(a, dd_neg(b))


def dd_mul(a, b):
    p, e = two_prod(a[0], b[0])
    return quick_two_sum(p, e + (a[0] * b[1] + a[1] * b[0]))


def dd_div(a, b):
    q = a[0] / b[0]
    zero = jnp.zeros_like(q)
    r = dd_sub(a, dd_mul((q, zero), b))
    return quick_two_sum(q, r[0] / b[0])


def roll(x, shift, axis):
    return pltpu.roll(x, shift % x.shape[axis], axis)


def halo_peers():
    lon, band = lax.axis_index("lon"), lax.axis_index("lat")
    west, east = lax.rem(lon + NLONB - 1, NLONB), lax.rem(lon + 1, NLONB)
    first = 1 - jnp.minimum(band, 1)
    last = jnp.maximum(band, NBAND - 2) - (NBAND - 2)

    def across(index, pole):
        return lax.rem(index + pole * (NLONB // 2), NLONB)

    left_band, right_band = band - 1 + first, band + 1 - last
    beside = ((west, band), (east, band))
    left = tuple((across(i, first), left_band) for i in (lon, west, east))
    right = tuple((across(i, last), right_band) for i in (lon, west, east))
    return beside, left, right, first, last


def sum_peers():
    lon, band = lax.axis_index("lon"), lax.axis_index("lat")
    x, y_hi, z = lax.rem(lon, NX), lax.rem(lon // NX, NYH), lon // (NX * NYH)
    core, y_lo = lax.rem(band, NC), band // NC
    me_a = (y_hi * NYL + y_lo) * NX + x
    me_b = z * NC + core

    def peer_a(j):
        t = lax.rem(me_a + j, SIZE_A)
        px, py = lax.rem(t, NX), t // NX
        return (z * NYH + py // NYL) * NX + px, lax.rem(py, NYL) * NC + core

    def peer_b(j):
        t = lax.rem(me_b + j, SIZE_B)
        pc, pz = lax.rem(t, NC), t // NC
        return (pz * NYH + y_hi) * NX + x, y_lo * NC + pc

    return (me_a, peer_a), (me_b, peer_b)


def repeat(start, stop, step):
    def one(j, carry):
        step(j)
        return carry

    lax.fori_loop(start, stop, one, 0)


def kernel(
    b_hbm, x_hbm, d_hbm, h_hbm, vc_hbm, sol_ref, res_ref,
    b_in, x_in, dh, dh_c, dh_o, q_a, q_b, q_n, o_n,
    near, wide, vs, packed, ext1, ext2, ex, ey, ring, moments, sums_a, sums_b, row_a, row_b, vc, couple,
    load_sem, send1, recv1, send1x, recv1x, send2, recv2, send2x, recv2x, send_a, recv_a, send_b, recv_b,
):
    beside, left, right, first, last = halo_peers()
    (me_a, peer_a), (me_b, peer_b) = sum_peers()

    loads = [
        pltpu.make_async_copy(src, dst.at[pl.ds(0, LEV), pl.ds(2, ROWS)], load_sem.at[i])
        for i, (src, dst) in enumerate(((d_hbm, dh.at[0]), (x_hbm, x_in), (h_hbm, dh.at[1]), (b_hbm, b_in)))
    ]
    loads.append(pltpu.make_async_copy(vc_hbm, vc, load_sem.at[4]))
    for copy in loads:
        copy.start()

    barrier = pltpu.get_barrier_semaphore()

    def greet(peer):
        pl.semaphore_signal(barrier, inc=1, device_id=peer, device_id_type=MESH)

    for peer in (*beside, *left, *right):
        greet(peer)
    for j in range(1, SIZE_B):
        greet(peer_b(j))
    for j in range(1, SIZE_A):
        greet(peer_a(j))

    lane = lax.broadcasted_iota(jnp.int32, (8, 128), 1)
    sub = lax.broadcasted_iota(jnp.int32, (8, 128), 0)
    lane5 = lax.broadcasted_iota(jnp.int32, (GROUPS, 8, 128), 2)
    sub5 = lax.broadcasted_iota(jnp.int32, (GROUPS, 8, 128), 1)
    col5 = lax.rem(lane5, 8)
    lane8 = lane // 8
    is_own = (sub >= 2) & (sub < 6)

    tail = jnp.zeros((PAD - LEV, 8, 128), F32)
    for ref in (b_in, x_in, near, dh.at[0], dh.at[1]):
        ref[LEV:PAD] = tail
    for i in range(3):
        for j in range(2):
            wide[i, j, LEV:PAD] = tail
    for ref in (q_a, q_b, q_n.at[0], q_n.at[1], o_n.at[0], o_n.at[1]):
        ref[0] = jnp.zeros((8, 128), F32)
        ref[PAD + 1] = jnp.zeros((8, 128), F32)

    def levels(step, init):
        def group(p, carry):
            return step(p, carry)

        return lax.fori_loop(0, GROUPS, group, init)

    def pack_in(tile, value, i):
        return jnp.where(lane8 == i, roll(value, 8 * i + 4, 1), tile)

    loads[0].wait()
    loads[1].wait()

    def scaled_guess(p, _):
        tile = jnp.zeros((8, 128), F32)
        for i in range(GROUP):
            k = p * GROUP + i
            value = dh[0, k] * x_in[k]
            q_a[k + 1] = value
            tile = pack_in(tile, value, i)
        packed[0, p] = tile
        return 0

    levels(scaled_guess, 0)

    def remote(src, dst, send, recv, peer):
        copy = pltpu.make_async_remote_copy(
            src_ref=src, dst_ref=dst, send_sem=send, recv_sem=recv, device_id=peer, device_id_type=MESH
        )
        copy.start()
        sends.append(copy)

    def landed(ref, sem):
        pltpu.make_async_copy(ref, ref, sem).wait()

    sends = []
    pl.semaphore_wait(barrier, 8 + SIZE_A - 1 + SIZE_B - 1)

    lev = pl.ds(0, LEV)
    lev1 = pl.ds(1, LEV)
    (west, east) = beside
    left_side, right_side = 1 - first, last
    remote(q_a.at[lev1, pl.ds(5, 1)], near.at[lev, pl.ds(5, 1)], send1.at[0], recv1.at[0], east)
    remote(q_a.at[lev1, pl.ds(2, 1)], near.at[lev, pl.ds(2, 1)], send1.at[1], recv1.at[1], west)
    mine = (slice(None), pl.ds(2, ROWS))
    remote(packed.at[0, *mine], ext1.at[left_side, *mine], send1x.at[0], recv1x.at[left_side], left[0])
    remote(packed.at[0, *mine], ext1.at[right_side, *mine], send1x.at[1], recv1x.at[right_side], right[0])

    def ring_rows(slot, at):
        deep = 2 if slot < 2 else 3
        return slice(None), (pl.ds(2, ROWS), pl.ds(6 - deep, deep), pl.ds(2, deep))[at]

    def send_packed(slot):
        for j in (1, 2, 0):
            at = (0, 2, 1)[j]
            rows = ring_rows(slot, at)
            remote(packed.at[slot + 1, *rows], ext2.at[slot, left_side, at, *rows], send2x.at[slot, 0, j],
                   recv2x.at[slot, left_side, at], left[j])
            remote(packed.at[slot + 1, *rows], ext2.at[slot, right_side, at, *rows], send2x.at[slot, 1, j],
                   recv2x.at[slot, right_side, at], right[j])

    loads[2].wait()
    for slot in range(2):
        remote(dh.at[slot, lev, pl.ds(3, 3)], wide.at[slot, 0, lev, pl.ds(3, 3)], send2.at[slot, 0],
               recv2.at[slot, 0], east)
        remote(dh.at[slot, lev, pl.ds(2, 3)], wide.at[slot, 1, lev, pl.ds(2, 3)], send2.at[slot, 1],
               recv2.at[slot, 1], west)

    def pack_coefficients(s):
        slot, p = s // GROUPS, lax.rem(s, GROUPS)
        tile = jnp.zeros((8, 128), F32)
        for i in range(GROUP):
            tile = pack_in(tile, dh[slot, p * GROUP + i], i)
        packed[slot + 1, p] = tile

    repeat(0, 2 * GROUPS, pack_coefficients)
    for slot in range(2):
        send_packed(slot)

    loads[4].wait()
    couple[0] = jnp.float32(0.0)

    def couple_in(k):
        couple[k] = vc[k - 1]

    def couple_none(k):
        couple[k] = jnp.float32(0.0)

    repeat(1, LEV, couple_in)
    repeat(LEV, PAD + 2, couple_none)

    def couple_tiles(p):
        below = jnp.zeros((8, 128), F32)
        above = jnp.zeros((8, 128), F32)
        for i in range(GROUP):
            k = p * GROUP + i
            here = lane8 == i
            below = jnp.where(here, couple[k + 1], below)
            above = jnp.where(here, couple[k], above)
        ey[1, p] = below
        ey[2, p] = above

    repeat(0, GROUPS, couple_tiles)

    def mirrored(value, side):
        if side == 0:
            out = roll(value, -1, 2)
            for c, s in ((0, -7), (1, -5), (2, -3)):
                out = jnp.where(col5 == c, roll(value, s, 2), out)
            return jnp.where(jnp.full(value.shape, first, jnp.int32) == 1, out, value)
        out = roll(value, 1, 2)
        for c, s in ((5, 3), (6, 5), (7, 7)):
            out = jnp.where(col5 == c, roll(value, s, 2), out)
        return jnp.where(jnp.full(value.shape, last, jnp.int32) == 1, out, value)

    def both_sides(part):
        return jnp.where(col5 < 4, mirrored(part(0), 0), mirrored(part(1), 1))

    def ring_center(slot):
        def part(side):
            lo, hi = roll(ext2[slot, side, 1], 4, 1), roll(ext2[slot, side, 2], 4, 1)
            return jnp.where(sub5 < 2, lo, jnp.where(sub5 >= 6, hi, ext2[slot, side, 0]))

        return both_sides(part)

    def ring_outer(slot):
        def part(side):
            lo, hi = roll(ext2[slot, side, 1], 4, 1), roll(ext2[slot, side, 2], 4, 1)
            return jnp.where(sub5 < 2, hi, lo)

        return both_sides(part)

    def edges(value):
        return jnp.where(col5 == 3, roll(value, -1, 2), roll(value, 1, 2))

    def lat_sum(q, edge, i):
        e = roll(edge, 124 - 8 * i, 1)
        return jnp.where(lane == 0, e, roll(q, 1, 1)) + jnp.where(lane == 127, e, roll(q, -1, 1))

    def stencil(q, below, above, h4, lon_sum, lat):
        return h4 * q - lon_sum - lat + (below - above)

    landed(near.at[lev, pl.ds(5, 1)], recv1.at[0])
    landed(near.at[lev, pl.ds(2, 1)], recv1.at[1])
    landed(ext1.at[0, *mine], recv1x.at[0])
    landed(ext1.at[1, *mine], recv1x.at[1])
    ey[0] = edges(both_sides(lambda side: ext1[side]))
    loads[3].wait()

    def first_residual(p, acc):
        acc, above = acc
        tile = jnp.zeros((8, 128), F32)
        edge = ey[0, p]
        for i in range(GROUP):
            k = p * GROUP + i
            q = q_a[k + 1]
            n = roll(near[k], 4, 0)
            lon_sum = roll(jnp.where(sub == 6, n, q), -1, 0) + roll(jnp.where(sub == 1, n, q), 1, 0)
            d = dh[0, k]
            below = couple[k + 1] * (q - q_a[k + 2])
            t = stencil(q, below, above, 4.0 + dh[1, k], lon_sum, lat_sum(q, edge, i))
            above = below
            r = b_in[k] - d * t
            vs[0, k] = r
            acc = acc + r * r
            value = d * r
            q_b[k + 1] = value
            tile = pack_in(tile, value, i)
        packed[3, p] = tile
        return acc, above

    zero = jnp.zeros((8, 128), F32)
    moments[0], _ = levels(first_residual, (zero, zero))

    send_packed(2)
    remote(q_b.at[lev1, pl.ds(2, ROWS)], wide.at[2, 0, lev, pl.ds(2, ROWS)], send2.at[2, 0], recv2.at[2, 0], east)
    remote(q_b.at[lev1, pl.ds(2, ROWS)], wide.at[2, 1, lev, pl.ds(2, ROWS)], send2.at[2, 1], recv2.at[2, 1], west)

    def wait_ring(slot):
        east_rows, west_rows = (pl.ds(3, 3), pl.ds(2, 3)) if slot < 2 else (pl.ds(2, ROWS),) * 2
        landed(wide.at[slot, 0, lev, east_rows], recv2.at[slot, 0])
        landed(wide.at[slot, 1, lev, west_rows], recv2.at[slot, 1])
        for side in range(2):
            for j in range(3):
                landed(ext2.at[slot, side, j, *ring_rows(slot, j)], recv2x.at[slot, side, j])

    def ring_and_mine(slot, k, mine):
        w, e = roll(wide[slot, 0, k], 4, 0), roll(wide[slot, 1, k], 4, 0)
        return jnp.where(sub < 2, w, jnp.where(sub >= 6, e, mine)), jnp.where(sub < 2, e, w)

    def gather_coefficients(s):
        slot, p = s // (PAD // 8), lax.rem(s, PAD // 8)
        plus = 4.0 * slot.astype(F32)
        for i in range(8):
            k = p * 8 + i
            center, outer = ring_and_mine(slot, k, dh[slot, k])
            dh_c[slot, k] = center + plus
            dh_o[slot, k] = outer + plus

    def gather_field(p):
        tile = jnp.zeros((8, 128), F32)
        for i in range(GROUP):
            k = p * GROUP + i
            center, outer = ring_and_mine(2, k, q_b[k + 1])
            q_n[0, k + 1] = center
            o_n[0, k + 1] = outer
            tile = pack_in(tile, center, i)
        ex[2, p] = tile

    wait_ring(0)
    wait_ring(1)
    repeat(0, 2 * (PAD // 8), gather_coefficients)
    ex[0] = ring_center(0)
    ex[1] = ring_center(1) + 4.0
    wait_ring(2)
    repeat(0, GROUPS, gather_field)
    ring[...] = ring_center(2)
    ring_o = ring_outer(2)
    ey[0] = edges(ring[...])
    ey[3] = edges(ring_o)
    ex[4] = ring_o

    def ring_step(x, edge_tiles, outer):
        right_of = roll(jnp.where(col5 == 4, edge_tiles, x), -1, 2)
        left_of = roll(jnp.where(col5 == 3, edge_tiles, x), 1, 2)
        o = outer
        lon_sum = roll(jnp.where(sub5 == 0, o, x), -1, 1) + roll(jnp.where(sub5 == 7, o, x), 1, 1)
        ahead, behind = roll(x, -8, 2), roll(x, 8, 2)
        none = jnp.zeros((1, 8, 128), F32)
        down = jnp.where(lane5 >= 120, jnp.concatenate([ahead[1:], none]), ahead)
        up = jnp.where(lane5 < 8, jnp.concatenate([none, behind[:-1]]), behind)
        t = ex[1] * x - lon_sum - (left_of + right_of) + (ey[1] * (x - down) - ey[2] * (up - x))
        d = ex[0]
        return d * (d * t)

    def outer_step(p):
        out = []
        edge = ey[3, p]
        above = couple[p * GROUP] * (o_n[0, p * GROUP] - o_n[0, p * GROUP + 1])
        for i in range(GROUP):
            k = p * GROUP + i
            o, q = o_n[0, k + 1], q_n[0, k + 1]
            lon_sum = roll(jnp.where(sub == 0, q, o), -1, 0) + roll(jnp.where(sub == 7, q, o), 1, 0)
            d = dh_o[0, k]
            below = couple[k + 1] * (o - o_n[0, k + 2])
            t = stencil(o, below, above, dh_o[1, k], lon_sum, lat_sum(o, edge, i))
            above = below
            out.append(d * (d * t))
        for i in range(GROUP):
            o_n[1, p * GROUP + i + 1] = out[i]

    repeat(0, GROUPS, outer_step)

    def packed_group(slot, p):
        tile = jnp.zeros((8, 128), F32)
        for i in range(GROUP):
            tile = pack_in(tile, q_n[slot, p * GROUP + i + 1], i)
        return tile

    def apply(n):
        src, dst = lax.rem(n + 1, 2), lax.rem(n, 2)
        beyond = jnp.minimum(n - 1, 1)

        def step(p, acc):
            even, odd, above = acc
            edge = ey[0, p]
            out = []
            before = jnp.maximum(p - 1, 0)
            ex[2 + dst, before] = packed_group(dst, before)
            for i in range(GROUP):
                k = p * GROUP + i
                q, o = q_n[src, k + 1], o_n[beyond, k + 1]
                lon_sum = roll(jnp.where(sub == 0, o, q), -1, 0) + roll(jnp.where(sub == 7, o, q), 1, 0)
                d = dh_c[0, k]
                below = couple[k + 1] * (q - q_n[src, k + 2])
                v = d * stencil(q, below, above, dh_c[1, k], lon_sum, lat_sum(q, edge, i))
                above = below
                odd = odd + vs[n - 1, k] * v
                even = even + v * v
                out.append((v, d * v))
            for i in range(GROUP):
                k = p * GROUP + i
                vs[n, k], q_n[dst, k + 1] = out[i]
            return even, odd, above

        even, odd, _ = levels(step, (zero, zero, zero))
        ex[2 + dst, GROUPS - 1] = packed_group(dst, GROUPS - 1)
        moments[2 * n - 1] = odd
        moments[2 * n] = even

        @pl.when(n < 4)
        def _():
            value = ring_step(ring[...], ex[2 + src], ex[4])
            ring[...] = value
            ey[0] = edges(value)

    repeat(1, 5, apply)

    def total(acc):
        value = jnp.where(is_own, acc, 0.0)
        pair = two_sum(value, roll(value, -2, 0))
        return dd_add(pair, tuple(roll(part, -1, 0) for part in pair))

    pairs = [total(moments[k]) for k in range(9)]
    row = jnp.zeros((8, 128), F32)
    for start in (0, 8):
        high, low = zero, zero
        for k in range(start, min(start + 8, len(pairs))):
            shift = k - start - 2
            high = jnp.where(sub == k - start, roll(pairs[k][0], shift, 0), high)
            low = jnp.where(sub == k - start, roll(pairs[k][1], shift, 0), low)
        pair = (high, low)
        for width in (64, 32, 16, 8, 4, 2, 1):
            pair = dd_add(pair, tuple(roll(part, width, 1) for part in pair))
        row = row + jnp.where(lane == sub + start, pair[0], 0.0) + jnp.where(lane == sub + start + 16, pair[1], 0.0)
    for width in (4, 2, 1):
        row = row + roll(row, width, 0)

    def sum_over(row, line, slots, me, peer, size, send, recv):
        line[...] = row
        slots[pl.ds(me, 1), :] = row[0:1]

        def give(j):
            copy = pltpu.make_async_remote_copy(
                src_ref=line.at[pl.ds(0, 1)], dst_ref=slots.at[pl.ds(me, 1)], send_sem=send.at[0],
                recv_sem=recv.at[0], device_id=peer(j), device_id_type=MESH,
            )
            copy.start()

        for j in range(1, size):
            give(j)
        landed(slots.at[pl.ds(0, size - 1)], recv.at[0])
        parts = [(slots[8 * j : 8 * j + 8], zero) for j in range(size // 8)]
        while len(parts) > 1:
            parts = [
                dd_add_raw(parts[j], parts[j + 1]) if j + 1 < len(parts) else parts[j] for j in range(0, len(parts), 2)
            ]
        pair = parts[0]
        for width in (4, 2, 1):
            pair = dd_add_raw(pair, tuple(roll(part, width, 0) for part in pair))
        low = pair[1] + roll(pair[0], -16, 1)
        high, low = quick_two_sum(pair[0], low)
        return jnp.where(lane < 16, high, jnp.where(lane < 32, roll(low, 16, 1), 0.0))

    def dd_add_raw(a, b):
        s, e = two_sum(a[0], b[0])
        return s, e + (a[1] + b[1])

    row = sum_over(row, row_a, sums_a, me_a, peer_a, SIZE_A, send_a, recv_a)
    row = sum_over(row, row_b, sums_b, me_b, peer_b, SIZE_B, send_b, recv_b)

    m = (row, roll(row, -16, 1))

    def at(pair, k):
        return tuple(jnp.broadcast_to(part[:, k : k + 1], (8, 128)) for part in pair)

    def ahead(pair, k):
        return tuple(roll(part, -k, 1) for part in pair)

    one = (jnp.ones((8, 128), F32), zero)
    m0, m1, m2, m3 = (at(m, k) for k in range(4))
    alpha = dd_div(m0, m1)
    g = dd_sub(m, dd_mul(alpha, ahead(m, 1)))
    t = dd_sub(g, dd_mul(alpha, ahead(g, 1)))
    omega = dd_div(at(t, 1), at(t, 2))
    rho = dd_sub(at(g, 0), dd_mul(omega, at(g, 1)))
    beta = dd_mul(dd_div(rho, m0), dd_div(alpha, omega))
    both = dd_add(alpha, omega)
    d0 = dd_add(one, beta)
    d1 = dd_neg(dd_add(both, dd_mul(beta, omega)))
    d2 = dd_mul(alpha, omega)
    image = dd_add(dd_add(dd_mul(d0, m1), dd_mul(d1, m2)), dd_mul(d2, m3))
    alpha1 = dd_div(rho, image)
    h1 = dd_neg(dd_add(both, dd_mul(alpha1, d0)))
    h2 = dd_sub(d2, dd_mul(alpha1, d1))
    h3 = dd_neg(dd_mul(alpha1, d2))

    def half_with(pair):
        out = pair
        for j, h in ((1, h1), (2, h2), (3, h3)):
            out = dd_add(out, dd_mul(h, ahead(pair, j)))
        return out

    t = half_with(half_with(m))
    omega1 = dd_div(at(t, 1), at(t, 2))
    res_c = (
        one,
        dd_sub(h1, omega1),
        dd_sub(h2, dd_mul(omega1, h1)),
        dd_sub(h3, dd_mul(omega1, h2)),
        dd_neg(dd_mul(omega1, h3)),
    )
    sol_c = (
        dd_add(dd_add(both, dd_mul(alpha1, d0)), omega1),
        dd_add(dd_sub(dd_mul(alpha1, d1), d2), dd_mul(omega1, h1)),
        dd_add(dd_mul(alpha1, d2), dd_mul(omega1, h2)),
        dd_mul(omega1, h3),
    )

    def finish(p):
        for i in range(7):
            k = p * 7 + i
            v = [vs[n, k] for n in range(5)]
            moved = sol_c[0][0] * v[0] + sol_c[1][0] * v[1] + sol_c[2][0] * v[2] + sol_c[3][0] * v[3]
            left_over = res_c[1][0] * v[1] + res_c[2][0] * v[2] + res_c[3][0] * v[3] + res_c[4][0] * v[4]
            sol_ref[k] = (x_in[k] + moved)[2:6]
            res_ref[k] = (v[0] + left_over)[2:6]

    repeat(0, LEV // 7, finish)
    for copy in sends:
        copy.wait_send()
    landed(sums_a.at[pl.ds(0, SIZE_A - 1)], send_a.at[0])
    landed(sums_b.at[pl.ds(0, SIZE_B - 1)], send_b.at[0])


def body(right_side, first_guess, cell_scale, helmholtz_term, vertical_coupling):
    block = jax.ShapeDtypeStruct((LEV, ROWS, 128), F32)
    field = pltpu.VMEM((PAD, 8, 128), F32)
    guarded = pltpu.VMEM((PAD + 2, 8, 128), F32)
    dma = pltpu.SemaphoreType.DMA
    return pl.pallas_call(
        kernel,
        out_shape=(block, block),
        in_specs=[pl.BlockSpec(memory_space=pltpu.HBM)] * 5,
        out_specs=(pl.BlockSpec(memory_space=pltpu.VMEM),) * 2,
        scratch_shapes=[
            field,
            field,
            *[pltpu.VMEM((2, PAD, 8, 128), F32)] * 3,
            guarded,
            guarded,
            *[pltpu.VMEM((2, PAD + 2, 8, 128), F32)] * 2,
            field,
            pltpu.VMEM((3, 2, PAD, 8, 128), F32),
            pltpu.VMEM((5, PAD, 8, 128), F32),
            pltpu.VMEM((4, GROUPS, 8, 128), F32),
            pltpu.VMEM((2, GROUPS, 8, 128), F32),
            pltpu.VMEM((3, 2, 3, GROUPS, 8, 128), F32),
            pltpu.VMEM((5, GROUPS, 8, 128), F32),
            pltpu.VMEM((4, GROUPS, 8, 128), F32),
            pltpu.VMEM((GROUPS, 8, 128), F32),
            pltpu.VMEM((9, 8, 128), F32),
            pltpu.VMEM((SIZE_A, 128), F32),
            pltpu.VMEM((SIZE_B, 128), F32),
            pltpu.VMEM((8, 128), F32),
            pltpu.VMEM((8, 128), F32),
            pltpu.SMEM((LEV - 1,), F32),
            pltpu.SMEM((PAD + 2,), F32),
            dma((5,)),
            dma((2,)),
            dma((2,)),
            dma((2,)),
            dma((2,)),
            dma((3, 2)),
            dma((3, 2)),
            dma((3, 2, 3)),
            dma((3, 2, 3)),
            *[dma((1,))] * 4,
        ],
        compiler_params=pltpu.CompilerParams(collective_id=0, has_side_effects=True, vmem_limit_bytes=54920 << 10),
        cost_estimate=pl.CostEstimate(flops=8_000_000, bytes_accessed=900_000, transcendentals=0),
    )(right_side, first_guess, cell_scale, helmholtz_term, vertical_coupling)


def solution(mesh):
    spec = P(None, "lon", "lat")
    return jax.shard_map(
        body, mesh=mesh, in_specs=(spec, spec, spec, spec, P()), out_specs=(spec, spec), check_vma=False
    )
```

```python
import jax
import jax.numpy as jnp
from jax import lax
from jax.experimental import pallas as pl
from jax.experimental.pallas import tpu as pltpu
from jax.sharding import PartitionSpec as P

MESH = pl.DeviceIdType.MESH
F32 = jnp.float32

LEV = 70
GROUP = 16
GROUPS = 5
PAD = GROUP * GROUPS
ROWS = 4
NX, NYH, NZ, NYL, NC = 4, 2, 12, 4, 2
NLONB, NBAND = NX * NYH * NZ, NYL * NC
SIZE_A, SIZE_B = NX * NYH * NYL, NZ * NC


def two_sum(a, b):
    s = a + b
    t = s - a
    return s, (a - (s - t)) + (b - t)


def quick_two_sum(a, b):
    s = a + b
    return s, b - (s - a)


def split(a):
    c = 4097.0 * a
    high = c - (c - a)
    return high, a - high


def two_prod(a, b):
    p = a * b
    ah, al = split(a)
    bh, bl = split(b)
    return p, ((ah * bh - p) + ah * bl + al * bh) + al * bl


def dd_add(a, b):
    s, e = two_sum(a[0], b[0])
    return quick_two_sum(s, e + (a[1] + b[1]))


def dd_neg(a):
    return -a[0], -a[1]


def dd_sub(a, b):
    return dd_add(a, dd_neg(b))


def dd_mul(a, b):
    p, e = two_prod(a[0], b[0])
    return quick_two_sum(p, e + (a[0] * b[1] + a[1] * b[0]))


def dd_div(a, b):
    q = a[0] / b[0]
    zero = jnp.zeros_like(q)
    r = dd_sub(a, dd_mul((q, zero), b))
    return quick_two_sum(q, r[0] / b[0])


def roll(x, shift, axis):
    return pltpu.roll(x, shift % x.shape[axis], axis)


def halo_peers():
    lon, band = lax.axis_index("lon"), lax.axis_index("lat")
    west, east = lax.rem(lon + NLONB - 1, NLONB), lax.rem(lon + 1, NLONB)
    first = 1 - jnp.minimum(band, 1)
    last = jnp.maximum(band, NBAND - 2) - (NBAND - 2)

    def across(index, pole):
        return lax.rem(index + pole * (NLONB // 2), NLONB)

    left_band, right_band = band - 1 + first, band + 1 - last
    beside = ((west, band), (east, band))
    left = tuple((across(i, first), left_band) for i in (lon, west, east))
    right = tuple((across(i, last), right_band) for i in (lon, west, east))
    return beside, left, right, first, last


def sum_peers():
    lon, band = lax.axis_index("lon"), lax.axis_index("lat")
    x, y_hi, z = lax.rem(lon, NX), lax.rem(lon // NX, NYH), lon // (NX * NYH)
    core, y_lo = lax.rem(band, NC), band // NC
    me_a = (y_hi * NYL + y_lo) * NX + x
    me_b = z * NC + core

    def peer_a(j):
        t = lax.rem(me_a + j, SIZE_A)
        px, py = lax.rem(t, NX), t // NX
        return (z * NYH + py // NYL) * NX + px, lax.rem(py, NYL) * NC + core

    def peer_b(j):
        t = lax.rem(me_b + j, SIZE_B)
        pc, pz = lax.rem(t, NC), t // NC
        return (pz * NYH + y_hi) * NX + x, y_lo * NC + pc

    return (me_a, peer_a), (me_b, peer_b)


def repeat(start, stop, step):
    def one(j, carry):
        step(j)
        return carry

    lax.fori_loop(start, stop, one, 0)


def kernel(
    b_hbm, x_hbm, d_hbm, h_hbm, vc_hbm, sol_ref, res_ref,
    b_in, x_in, dh, dh_c, dh_o, q_a, q_b, q_n, o_n,
    near, wide, vs, packed, ext1, ext2, ex, ey, ring, moments, sums_a, sums_b, row_a, row_b, vc, couple,
    load_sem, send1, recv1, send1x, recv1x, send2, recv2, send2x, recv2x, send_a, recv_a, send_b, recv_b,
):
    beside, left, right, first, last = halo_peers()
    (me_a, peer_a), (me_b, peer_b) = sum_peers()

    loads = [
        pltpu.make_async_copy(src, dst.at[pl.ds(0, LEV), pl.ds(2, ROWS)], load_sem.at[i])
        for i, (src, dst) in enumerate(((d_hbm, dh.at[0]), (x_hbm, x_in), (h_hbm, dh.at[1]), (b_hbm, b_in)))
    ]
    loads.append(pltpu.make_async_copy(vc_hbm, vc, load_sem.at[4]))
    for copy in loads:
        copy.start()

    barrier = pltpu.get_barrier_semaphore()

    def greet(peer):
        pl.semaphore_signal(barrier, inc=1, device_id=peer, device_id_type=MESH)

    for peer in (*beside, *left, *right):
        greet(peer)
    for j in range(1, SIZE_B):
        greet(peer_b(j))
    for j in range(1, SIZE_A):
        greet(peer_a(j))

    lane = lax.broadcasted_iota(jnp.int32, (8, 128), 1)
    sub = lax.broadcasted_iota(jnp.int32, (8, 128), 0)
    lane5 = lax.broadcasted_iota(jnp.int32, (GROUPS, 8, 128), 2)
    sub5 = lax.broadcasted_iota(jnp.int32, (GROUPS, 8, 128), 1)
    col5 = lax.rem(lane5, 8)
    lane8 = lane // 8
    is_own = (sub >= 2) & (sub < 6)

    tail = jnp.zeros((PAD - LEV, 8, 128), F32)
    for ref in (b_in, x_in, near, dh.at[0], dh.at[1]):
        ref[LEV:PAD] = tail
    for i in range(3):
        for j in range(2):
            wide[i, j, LEV:PAD] = tail
    for ref in (q_a, q_b, q_n.at[0], q_n.at[1], o_n.at[0], o_n.at[1]):
        ref[0] = jnp.zeros((8, 128), F32)
        ref[PAD + 1] = jnp.zeros((8, 128), F32)

    def levels(step, init):
        def group(p, carry):
            return step(p, carry)

        return lax.fori_loop(0, GROUPS, group, init)

    def pack_in(tile, value, i):
        return jnp.where(lane8 == i, roll(value, 8 * i + 4, 1), tile)

    loads[0].wait()
    loads[1].wait()

    def scaled_guess(p, _):
        tile = jnp.zeros((8, 128), F32)
        for i in range(GROUP):
            k = p * GROUP + i
            value = dh[0, k] * x_in[k]
            q_a[k + 1] = value
            tile = pack_in(tile, value, i)
        packed[0, p] = tile
        return 0

    levels(scaled_guess, 0)

    def remote(src, dst, send, recv, peer):
        copy = pltpu.make_async_remote_copy(
            src_ref=src, dst_ref=dst, send_sem=send, recv_sem=recv, device_id=peer, device_id_type=MESH
        )
        copy.start()
        sends.append(copy)

    def landed(ref, sem):
        pltpu.make_async_copy(ref, ref, sem).wait()

    sends = []
    pl.semaphore_wait(barrier, 8 + SIZE_A - 1 + SIZE_B - 1)

    lev = pl.ds(0, LEV)
    lev1 = pl.ds(1, LEV)
    (west, east) = beside
    left_side, right_side = 1 - first, last
    remote(q_a.at[lev1, pl.ds(5, 1)], near.at[lev, pl.ds(5, 1)], send1.at[0], recv1.at[0], east)
    remote(q_a.at[lev1, pl.ds(2, 1)], near.at[lev, pl.ds(2, 1)], send1.at[1], recv1.at[1], west)
    mine = (slice(None), pl.ds(2, ROWS))
    remote(packed.at[0, *mine], ext1.at[left_side, *mine], send1x.at[0], recv1x.at[left_side], left[0])
    remote(packed.at[0, *mine], ext1.at[right_side, *mine], send1x.at[1], recv1x.at[right_side], right[0])

    def ring_rows(slot, at):
        deep = 2 if slot < 2 else 3
        return slice(None), (pl.ds(2, ROWS), pl.ds(6 - deep, deep), pl.ds(2, deep))[at]

    def send_packed(slot):
        for j in (1, 2, 0):
            at = (0, 2, 1)[j]
            rows = ring_rows(slot, at)
            remote(packed.at[slot + 1, *rows], ext2.at[slot, left_side, at, *rows], send2x.at[slot, 0, j],
                   recv2x.at[slot, left_side, at], left[j])
            remote(packed.at[slot + 1, *rows], ext2.at[slot, right_side, at, *rows], send2x.at[slot, 1, j],
                   recv2x.at[slot, right_side, at], right[j])

    loads[2].wait()
    for slot in range(2):
        remote(dh.at[slot, lev, pl.ds(3, 3)], wide.at[slot, 0, lev, pl.ds(3, 3)], send2.at[slot, 0],
               recv2.at[slot, 0], east)
        remote(dh.at[slot, lev, pl.ds(2, 3)], wide.at[slot, 1, lev, pl.ds(2, 3)], send2.at[slot, 1],
               recv2.at[slot, 1], west)

    def pack_coefficients(s):
        slot, p = s // GROUPS, lax.rem(s, GROUPS)
        tile = jnp.zeros((8, 128), F32)
        for i in range(GROUP):
            tile = pack_in(tile, dh[slot, p * GROUP + i], i)
        packed[slot + 1, p] = tile

    repeat(0, 2 * GROUPS, pack_coefficients)
    for slot in range(2):
        send_packed(slot)

    loads[4].wait()
    couple[0] = jnp.float32(0.0)

    def couple_in(k):
        couple[k] = vc[k - 1]

    def couple_none(k):
        couple[k] = jnp.float32(0.0)

    repeat(1, LEV, couple_in)
    repeat(LEV, PAD + 2, couple_none)

    def couple_tiles(p):
        below = jnp.zeros((8, 128), F32)
        above = jnp.zeros((8, 128), F32)
        for i in range(GROUP):
            k = p * GROUP + i
            here = lane8 == i
            below = jnp.where(here, couple[k + 1], below)
            above = jnp.where(here, couple[k], above)
        ey[1, p] = below
        ey[2, p] = above

    repeat(0, GROUPS, couple_tiles)

    def mirrored(value, side):
        if side == 0:
            out = roll(value, -1, 2)
            for c, s in ((0, -7), (1, -5), (2, -3)):
                out = jnp.where(col5 == c, roll(value, s, 2), out)
            return jnp.where(jnp.full(value.shape, first, jnp.int32) == 1, out, value)
        out = roll(value, 1, 2)
        for c, s in ((5, 3), (6, 5), (7, 7)):
            out = jnp.where(col5 == c, roll(value, s, 2), out)
        return jnp.where(jnp.full(value.shape, last, jnp.int32) == 1, out, value)

    def both_sides(part):
        return jnp.where(col5 < 4, mirrored(part(0), 0), mirrored(part(1), 1))

    def ring_center(slot):
        def part(side):
            lo, hi = roll(ext2[slot, side, 1], 4, 1), roll(ext2[slot, side, 2], 4, 1)
            return jnp.where(sub5 < 2, lo, jnp.where(sub5 >= 6, hi, ext2[slot, side, 0]))

        return both_sides(part)

    def ring_outer(slot):
        def part(side):
            lo, hi = roll(ext2[slot, side, 1], 4, 1), roll(ext2[slot, side, 2], 4, 1)
            return jnp.where(sub5 < 2, hi, lo)

        return both_sides(part)

    def edges(value):
        return jnp.where(col5 == 3, roll(value, -1, 2), roll(value, 1, 2))

    def lat_sum(q, edge, i):
        e = roll(edge, 124 - 8 * i, 1)
        return jnp.where(lane == 0, e, roll(q, 1, 1)) + jnp.where(lane == 127, e, roll(q, -1, 1))

    def stencil(q, below, above, h4, lon_sum, lat):
        return h4 * q - lon_sum - lat + (below - above)

    landed(near.at[lev, pl.ds(5, 1)], recv1.at[0])
    landed(near.at[lev, pl.ds(2, 1)], recv1.at[1])
    landed(ext1.at[0, *mine], recv1x.at[0])
    landed(ext1.at[1, *mine], recv1x.at[1])
    ey[0] = edges(both_sides(lambda side: ext1[side]))
    loads[3].wait()

    def first_residual(p, acc):
        acc, above = acc
        tile = jnp.zeros((8, 128), F32)
        edge = ey[0, p]
        for i in range(GROUP):
            k = p * GROUP + i
            q = q_a[k + 1]
            n = roll(near[k], 4, 0)
            lon_sum = roll(jnp.where(sub == 6, n, q), -1, 0) + roll(jnp.where(sub == 1, n, q), 1, 0)
            d = dh[0, k]
            below = couple[k + 1] * (q - q_a[k + 2])
            t = stencil(q, below, above, 4.0 + dh[1, k], lon_sum, lat_sum(q, edge, i))
            above = below
            r = b_in[k] - d * t
            vs[0, k] = r
            acc = acc + r * r
            value = d * r
            q_b[k + 1] = value
            tile = pack_in(tile, value, i)
        packed[3, p] = tile
        return acc, above

    zero = jnp.zeros((8, 128), F32)
    moments[0], _ = levels(first_residual, (zero, zero))

    send_packed(2)
    remote(q_b.at[lev1, pl.ds(2, ROWS)], wide.at[2, 0, lev, pl.ds(2, ROWS)], send2.at[2, 0], recv2.at[2, 0], east)
    remote(q_b.at[lev1, pl.ds(2, ROWS)], wide.at[2, 1, lev, pl.ds(2, ROWS)], send2.at[2, 1], recv2.at[2, 1], west)

    def wait_ring(slot):
        east_rows, west_rows = (pl.ds(3, 3), pl.ds(2, 3)) if slot < 2 else (pl.ds(2, ROWS),) * 2
        landed(wide.at[slot, 0, lev, east_rows], recv2.at[slot, 0])
        landed(wide.at[slot, 1, lev, west_rows], recv2.at[slot, 1])
        for side in range(2):
            for j in range(3):
                landed(ext2.at[slot, side, j, *ring_rows(slot, j)], recv2x.at[slot, side, j])

    def ring_and_mine(slot, k, mine):
        w, e = roll(wide[slot, 0, k], 4, 0), roll(wide[slot, 1, k], 4, 0)
        return jnp.where(sub < 2, w, jnp.where(sub >= 6, e, mine)), jnp.where(sub < 2, e, w)

    def gather_coefficients(s):
        slot, p = s // (PAD // 8), lax.rem(s, PAD // 8)
        plus = 4.0 * slot.astype(F32)
        for i in range(8):
            k = p * 8 + i
            center, outer = ring_and_mine(slot, k, dh[slot, k])
            dh_c[slot, k] = center + plus
            dh_o[slot, k] = outer + plus

    def gather_field(p):
        tile = jnp.zeros((8, 128), F32)
        for i in range(GROUP):
            k = p * GROUP + i
            center, outer = ring_and_mine(2, k, q_b[k + 1])
            q_n[0, k + 1] = center
            o_n[0, k + 1] = outer
            tile = pack_in(tile, center, i)
        ex[2, p] = tile

    wait_ring(0)
    wait_ring(1)
    repeat(0, 2 * (PAD // 8), gather_coefficients)
    ex[0] = ring_center(0)
    ex[1] = ring_center(1) + 4.0
    wait_ring(2)
    repeat(0, GROUPS, gather_field)
    ring[...] = ring_center(2)
    ring_o = ring_outer(2)
    ey[0] = edges(ring[...])
    ey[3] = edges(ring_o)
    ex[4] = ring_o

    def ring_step(x, edge_tiles, outer):
        right_of = roll(jnp.where(col5 == 4, edge_tiles, x), -1, 2)
        left_of = roll(jnp.where(col5 == 3, edge_tiles, x), 1, 2)
        o = outer
        lon_sum = roll(jnp.where(sub5 == 0, o, x), -1, 1) + roll(jnp.where(sub5 == 7, o, x), 1, 1)
        ahead, behind = roll(x, -8, 2), roll(x, 8, 2)
        none = jnp.zeros((1, 8, 128), F32)
        down = jnp.where(lane5 >= 120, jnp.concatenate([ahead[1:], none]), ahead)
        up = jnp.where(lane5 < 8, jnp.concatenate([none, behind[:-1]]), behind)
        t = ex[1] * x - lon_sum - (left_of + right_of) + (ey[1] * (x - down) - ey[2] * (up - x))
        d = ex[0]
        return d * (d * t)

    def outer_step(p):
        out = []
        edge = ey[3, p]
        above = couple[p * GROUP] * (o_n[0, p * GROUP] - o_n[0, p * GROUP + 1])
        for i in range(GROUP):
            k = p * GROUP + i
            o, q = o_n[0, k + 1], q_n[0, k + 1]
            lon_sum = roll(jnp.where(sub == 0, q, o), -1, 0) + roll(jnp.where(sub == 7, q, o), 1, 0)
            d = dh_o[0, k]
            below = couple[k + 1] * (o - o_n[0, k + 2])
            t = stencil(o, below, above, dh_o[1, k], lon_sum, lat_sum(o, edge, i))
            above = below
            out.append(d * (d * t))
        for i in range(GROUP):
            o_n[1, p * GROUP + i + 1] = out[i]

    repeat(0, GROUPS, outer_step)

    def packed_group(slot, p):
        tile = jnp.zeros((8, 128), F32)
        for i in range(GROUP):
            tile = pack_in(tile, q_n[slot, p * GROUP + i + 1], i)
        return tile

    def apply(n):
        src, dst = lax.rem(n + 1, 2), lax.rem(n, 2)
        beyond = jnp.minimum(n - 1, 1)

        def step(p, acc):
            even, odd, above = acc
            edge = ey[0, p]
            out = []
            before = jnp.maximum(p - 1, 0)
            ex[2 + dst, before] = packed_group(dst, before)
            for i in range(GROUP):
                k = p * GROUP + i
                q, o = q_n[src, k + 1], o_n[beyond, k + 1]
                lon_sum = roll(jnp.where(sub == 0, o, q), -1, 0) + roll(jnp.where(sub == 7, o, q), 1, 0)
                d = dh_c[0, k]
                below = couple[k + 1] * (q - q_n[src, k + 2])
                v = d * stencil(q, below, above, dh_c[1, k], lon_sum, lat_sum(q, edge, i))
                above = below
                odd = odd + vs[n - 1, k] * v
                even = even + v * v
                out.append((v, d * v))
            for i in range(GROUP):
                k = p * GROUP + i
                vs[n, k], q_n[dst, k + 1] = out[i]
            return even, odd, above

        even, odd, _ = lax.fori_loop(0, GROUPS, step, (zero, zero, zero), unroll=GROUPS)
        ex[2 + dst, GROUPS - 1] = packed_group(dst, GROUPS - 1)
        moments[2 * n - 1] = odd
        moments[2 * n] = even

        @pl.when(n < 4)
        def _():
            value = ring_step(ring[...], ex[2 + src], ex[4])
            ring[...] = value
            ey[0] = edges(value)

    repeat(1, 5, apply)

    def total(acc):
        value = jnp.where(is_own, acc, 0.0)
        pair = two_sum(value, roll(value, -2, 0))
        return dd_add(pair, tuple(roll(part, -1, 0) for part in pair))

    pairs = [total(moments[k]) for k in range(9)]
    row = jnp.zeros((8, 128), F32)
    for start in (0, 8):
        high, low = zero, zero
        for k in range(start, min(start + 8, len(pairs))):
            shift = k - start - 2
            high = jnp.where(sub == k - start, roll(pairs[k][0], shift, 0), high)
            low = jnp.where(sub == k - start, roll(pairs[k][1], shift, 0), low)
        pair = (high, low)
        for width in (64, 32, 16, 8, 4, 2, 1):
            pair = dd_add(pair, tuple(roll(part, width, 1) for part in pair))
        row = row + jnp.where(lane == sub + start, pair[0], 0.0) + jnp.where(lane == sub + start + 16, pair[1], 0.0)
    for width in (4, 2, 1):
        row = row + roll(row, width, 0)

    def sum_over(row, line, slots, me, peer, size, send, recv):
        line[...] = row
        slots[pl.ds(me, 1), :] = row[0:1]

        def give(j):
            copy = pltpu.make_async_remote_copy(
                src_ref=line.at[pl.ds(0, 1)], dst_ref=slots.at[pl.ds(me, 1)], send_sem=send.at[0],
                recv_sem=recv.at[0], device_id=peer(j), device_id_type=MESH,
            )
            copy.start()

        for j in range(1, size):
            give(j)
        landed(slots.at[pl.ds(0, size - 1)], recv.at[0])
        parts = [(slots[8 * j : 8 * j + 8], zero) for j in range(size // 8)]
        while len(parts) > 1:
            parts = [
                dd_add_raw(parts[j], parts[j + 1]) if j + 1 < len(parts) else parts[j] for j in range(0, len(parts), 2)
            ]
        pair = parts[0]
        for width in (4, 2, 1):
            pair = dd_add_raw(pair, tuple(roll(part, width, 0) for part in pair))
        low = pair[1] + roll(pair[0], -16, 1)
        high, low = quick_two_sum(pair[0], low)
        return jnp.where(lane < 16, high, jnp.where(lane < 32, roll(low, 16, 1), 0.0))

    def dd_add_raw(a, b):
        s, e = two_sum(a[0], b[0])
        return s, e + (a[1] + b[1])

    row = sum_over(row, row_a, sums_a, me_a, peer_a, SIZE_A, send_a, recv_a)
    row = sum_over(row, row_b, sums_b, me_b, peer_b, SIZE_B, send_b, recv_b)

    m = (row, roll(row, -16, 1))

    def at(pair, k):
        return tuple(jnp.broadcast_to(part[:, k : k + 1], (8, 128)) for part in pair)

    def ahead(pair, k):
        return tuple(roll(part, -k, 1) for part in pair)

    one = (jnp.ones((8, 128), F32), zero)
    m0, m1, m2, m3 = (at(m, k) for k in range(4))
    alpha = dd_div(m0, m1)
    g = dd_sub(m, dd_mul(alpha, ahead(m, 1)))
    t = dd_sub(g, dd_mul(alpha, ahead(g, 1)))
    omega = dd_div(at(t, 1), at(t, 2))
    rho = dd_sub(at(g, 0), dd_mul(omega, at(g, 1)))
    beta = dd_mul(dd_div(rho, m0), dd_div(alpha, omega))
    both = dd_add(alpha, omega)
    d0 = dd_add(one, beta)
    d1 = dd_neg(dd_add(both, dd_mul(beta, omega)))
    d2 = dd_mul(alpha, omega)
    image = dd_add(dd_add(dd_mul(d0, m1), dd_mul(d1, m2)), dd_mul(d2, m3))
    alpha1 = dd_div(rho, image)
    h1 = dd_neg(dd_add(both, dd_mul(alpha1, d0)))
    h2 = dd_sub(d2, dd_mul(alpha1, d1))
    h3 = dd_neg(dd_mul(alpha1, d2))

    def half_with(pair):
        out = pair
        for j, h in ((1, h1), (2, h2), (3, h3)):
            out = dd_add(out, dd_mul(h, ahead(pair, j)))
        return out

    t = half_with(half_with(m))
    omega1 = dd_div(at(t, 1), at(t, 2))
    res_c = (
        one,
        dd_sub(h1, omega1),
        dd_sub(h2, dd_mul(omega1, h1)),
        dd_sub(h3, dd_mul(omega1, h2)),
        dd_neg(dd_mul(omega1, h3)),
    )
    sol_c = (
        dd_add(dd_add(both, dd_mul(alpha1, d0)), omega1),
        dd_add(dd_sub(dd_mul(alpha1, d1), d2), dd_mul(omega1, h1)),
        dd_add(dd_mul(alpha1, d2), dd_mul(omega1, h2)),
        dd_mul(omega1, h3),
    )

    def finish(p):
        for i in range(7):
            k = p * 7 + i
            v = [vs[n, k] for n in range(5)]
            moved = sol_c[0][0] * v[0] + sol_c[1][0] * v[1] + sol_c[2][0] * v[2] + sol_c[3][0] * v[3]
            left_over = res_c[1][0] * v[1] + res_c[2][0] * v[2] + res_c[3][0] * v[3] + res_c[4][0] * v[4]
            sol_ref[k] = (x_in[k] + moved)[2:6]
            res_ref[k] = (v[0] + left_over)[2:6]

    repeat(0, LEV // 7, finish)
    for copy in sends:
        copy.wait_send()
    landed(sums_a.at[pl.ds(0, SIZE_A - 1)], send_a.at[0])
    landed(sums_b.at[pl.ds(0, SIZE_B - 1)], send_b.at[0])


def body(right_side, first_guess, cell_scale, helmholtz_term, vertical_coupling):
    block = jax.ShapeDtypeStruct((LEV, ROWS, 128), F32)
    field = pltpu.VMEM((PAD, 8, 128), F32)
    guarded = pltpu.VMEM((PAD + 2, 8, 128), F32)
    dma = pltpu.SemaphoreType.DMA
    return pl.pallas_call(
        kernel,
        out_shape=(block, block),
        in_specs=[pl.BlockSpec(memory_space=pltpu.HBM)] * 5,
        out_specs=(pl.BlockSpec(memory_space=pltpu.VMEM),) * 2,
        scratch_shapes=[
            field,
            field,
            *[pltpu.VMEM((2, PAD, 8, 128), F32)] * 3,
            guarded,
            guarded,
            *[pltpu.VMEM((2, PAD + 2, 8, 128), F32)] * 2,
            field,
            pltpu.VMEM((3, 2, PAD, 8, 128), F32),
            pltpu.VMEM((5, PAD, 8, 128), F32),
            pltpu.VMEM((4, GROUPS, 8, 128), F32),
            pltpu.VMEM((2, GROUPS, 8, 128), F32),
            pltpu.VMEM((3, 2, 3, GROUPS, 8, 128), F32),
            pltpu.VMEM((5, GROUPS, 8, 128), F32),
            pltpu.VMEM((4, GROUPS, 8, 128), F32),
            pltpu.VMEM((GROUPS, 8, 128), F32),
            pltpu.VMEM((9, 8, 128), F32),
            pltpu.VMEM((SIZE_A, 128), F32),
            pltpu.VMEM((SIZE_B, 128), F32),
            pltpu.VMEM((8, 128), F32),
            pltpu.VMEM((8, 128), F32),
            pltpu.SMEM((LEV - 1,), F32),
            pltpu.SMEM((PAD + 2,), F32),
            dma((5,)),
            dma((2,)),
            dma((2,)),
            dma((2,)),
            dma((2,)),
            dma((3, 2)),
            dma((3, 2)),
            dma((3, 2, 3)),
            dma((3, 2, 3)),
            *[dma((1,))] * 4,
        ],
        compiler_params=pltpu.CompilerParams(collective_id=0, has_side_effects=True, vmem_limit_bytes=54920 << 10),
        cost_estimate=pl.CostEstimate(flops=8_000_000, bytes_accessed=900_000, transcendentals=0),
    )(right_side, first_guess, cell_scale, helmholtz_term, vertical_coupling)


def solution(mesh):
    spec = P(None, "lon", "lat")
    return jax.shard_map(
        body, mesh=mesh, in_specs=(spec, spec, spec, spec, P()), out_specs=(spec, spec), check_vma=False
    )
```
